256 devices in a mesh: layer: 4 (over y_hi, core), rows: 4 (over x), feat: 16 (over z, y_lo).
Axes of the slice: x: 4, y: 4 (y_hi: 2, y_lo: 2; y = y_hi * 2 + y_lo), z: 8, core: 2. Of those that a mesh axis runs over, the one named last changes fastest.
Arguments:
- resid: bfloat16 [4, 512, 2304], P('layer', 'rows'), may hold values from -6 to 6
- norm_gain: float32 [4, 2304], P('layer'), may hold values from 0.5 to 2
- gate_weight: bfloat16 [4, 9216, 2304], P('layer', ('rows', 'feat')), may hold values from -0.125 to 0.125
- up_weight: bfloat16 [4, 9216, 2304], P('layer', ('rows', 'feat')), may hold values from -0.125 to 0.125
- down_weight: bfloat16 [4, 9216, 2304], P('layer', ('rows', 'feat')), may hold values from -0.0625 to 0.0625
- enc_weight: bfloat16 [4, 2304, 32768], P('layer', None, ('rows', 'feat')), may hold values from -0.125 to 0.125
- enc_bias: float32 [4, 32768], P('layer', ('rows', 'feat')), may hold values from -3 to 3
- dec_weight: bfloat16 [10, 32768, 2304], P(None, ('rows', 'feat'), 'layer'), may hold values from -0.03125 to 0.03125
- dec_bias: float32 [4, 2304], P(None, 'layer'), may hold values from -3 to 3
Outputs:
- errors: bfloat16 [512, 4, 2304], P(('rows', 'feat'), None, 'layer')
- act_grad: bfloat16 [4, 512, 32768], P('layer', None, ('rows', 'feat'))
The draws below stay inside these ranges and needn't reach their ends.
All inputs are finite; a program needn't handle non-finite values.
Results may differ from the reference program's by a relative error of at most 0.017.
Values may be sent and summed in bfloat16 or wider, within the bound.
A program may use at most 128 MiB of HBM per device.

```python
import math
import jax
import jax.numpy as jnp
from jax import lax

D = 2304
H = 9216
F = 32768
L = 4
TOKENS = 512
PAIRS = 10


def steps_of(key, extent, cuts, least, largest):
    loudness, own = 1.0, jax.random.fold_in(key, 6)
    for position, shards_of in cuts:
        heights = jnp.exp(jax.random.uniform(jax.random.fold_in(own, position), (shards_of,), jnp.float32, least / len(cuts), largest / len(cuts)))
        loudness = loudness * jnp.repeat(heights, extent[position] // shards_of).reshape([-1 if axis == position else 1 for axis in range(len(extent))])
    return loudness


def gaussian(own_key, dims, scale, bound, pieces=(), kind=jnp.bfloat16):
    result = scale * jax.random.normal(own_key, dims, jnp.float32)
    if pieces:
        result = result * steps_of(own_key, dims, pieces, -0.22, 0.18)
    return jnp.clip(result, -bound, bound).astype(kind)


def setup_inputs(seed: int = 0) -> dict:
    arg_keys = jax.random.split(jax.random.key(seed), 10)
    return {
        "resid": gaussian(arg_keys[0], (L, TOKENS, D), 1.0, 6.0, ((0, 4), (1, 4))),
        "norm_gain": jnp.clip(jnp.exp(math.log(2.0) - 1.3862944 * jax.random.uniform(arg_keys[1], (L, D), jnp.float32) ** steps_of(arg_keys[1], (L, D), ((0, 4),), -0.2, 0.2)), 0.5, 2.0),
        "gate_weight": gaussian(arg_keys[2], (L, H, D), D ** -0.5, 0.125, ((0, 4), (1, 64))),
        "up_weight": gaussian(arg_keys[3], (L, H, D), D ** -0.5, 0.125, ((0, 4), (1, 64))),
        "down_weight": gaussian(arg_keys[4], (L, H, D), H ** -0.5, 0.0625, ((0, 4), (1, 64))),
        "enc_weight": gaussian(arg_keys[5], (L, D, F), D ** -0.5, 0.125, ((0, 4), (2, 64))),
        "enc_bias": gaussian(arg_keys[6], (L, F), 0.5, 3.0, ((0, 4), (1, 64)), jnp.float32),
        "dec_weight": gaussian(arg_keys[7], (PAIRS, F, D), F ** -0.5, 0.03125, ((1, 64), (2, 4))),
        "dec_bias": gaussian(arg_keys[8], (L, D), 0.5, 3.0, ((1, 4),), jnp.float32),
    }


def pair_index(source, target, layers):
    return source * layers - source * (source - 1) // 2 + target - source

def normalize(resid_rows, gain_row):
    as_float = resid_rows.astype(jnp.float32)
    inv_rms = lax.rsqrt(lax.optimization_barrier(jnp.mean(as_float * as_float, axis=-1, keepdims=True)) + 1e-06)
    return (as_float * inv_rms * gain_row).astype(jnp.bfloat16)

def reference(resid, norm_gain, gate_weight, up_weight, down_weight, enc_weight, enc_bias, dec_weight, dec_bias):
    layers = resid.shape[0]
    features = []
    mlp_outs = []
    for layer_idx in range(layers):
        normed = normalize(resid[layer_idx], norm_gain[layer_idx])
        gate_proj = jnp.dot(normed, gate_weight[layer_idx].T, preferred_element_type=jnp.float32)
        up_proj = jnp.dot(normed, up_weight[layer_idx].T, preferred_element_type=jnp.float32)
        hidden = (jax.nn.gelu(gate_proj, approximate=True) * up_proj).astype(jnp.bfloat16)
        mlp_outs.append(jnp.dot(hidden, down_weight[layer_idx], preferred_element_type=jnp.float32))
        pre_act = jnp.dot(normed, enc_weight[layer_idx], preferred_element_type=jnp.float32) + enc_bias[layer_idx]
        features.append(jnp.maximum(pre_act, 0.0).astype(jnp.bfloat16))
    error_list = []
    for target in range(layers):
        running = dec_bias[target] - mlp_outs[target]
        for source in range(target + 1):
            running = running + jnp.dot(features[source], dec_weight[pair_index(source, target, layers)], preferred_element_type=jnp.float32)
        error_list.append(running.astype(jnp.bfloat16))
    gradients = []
    for source in range(layers):
        running = jnp.zeros((resid.shape[1], enc_weight.shape[2]), jnp.float32)
        for target in range(source, layers):
            running = running + jnp.dot(error_list[target], dec_weight[pair_index(source, target, layers)].T, preferred_element_type=jnp.float32)
        gradients.append(running.astype(jnp.bfloat16))
    return (jnp.stack(error_list, 1), jnp.stack(gradients, 0))
```

```python
import jax
import jax.numpy as jnp
from jax import lax
from jax.experimental import pallas as pl
from jax.experimental.pallas import tpu as pltpu
from jax.sharding import PartitionSpec as P

MESH = pl.DeviceIdType.MESH
BF16 = jnp.bfloat16
F32 = jnp.float32


def pair_index(source, target, layers=4):
    return source * layers - source * (source - 1) // 2 + target - source


def dot(left, right):
    return lax.dot_general(left, right, (((1,), (0,)), ((), ())), preferred_element_type=F32)


def dot_t(left, right):
    return lax.dot_general(left, right, (((1,), (1,)), ((), ())), preferred_element_type=F32)


def gelu(x):
    inner = 0.7978845608028654 * (x + 0.044715 * (x * x * x))
    return 0.5 * x * (1.0 + jnp.tanh(inner))


def kernel(
    resid, gain, gate_w, up_w, down_w, enc_w, enc_b, dec_w, dec_b,
    err_out, act_out,
    res_v, xg, ew, gw, uw, dw, wsend, wd, dv, fh,
    xs, own, xr, zf, zs, zr, ps, pr, ef, eg, acc, gs, ga, gt, gb,
    load_sem, w_ss, w_rs, xa_ss, xa_rs, zf_ss, zf_rs, fc_ss, fc_rs, fy_ss, fy_rs, ff_ss, ff_rs,
    x_ss, x_rs, z_ss, z_rs, p_ss, p_rs, az_ss, az_rs, ax_ss, ax_rs, gc_ss, gc_rs, gy_ss, gy_rs,
):
    l, r, f = lax.axis_index("layer"), lax.axis_index("rows"), lax.axis_index("feat")
    yh, c = l // 2, l % 2
    z, yl = f // 2, f % 2
    half = z % 2
    other = 1 - half

    def x_peer(d):
        return (l, (r + d) % 4, f)

    def z_peer(d):
        return (l, r, ((z + d) % 8) * 2 + yl)

    y_pair = (l, r, z * 2 + (1 - yl))
    core_l = yh * 2 + (1 - c)
    far_l = (1 - yh) * 2 + c
    cross_l = (1 - yh) * 2 + (1 - c)
    core_peer, far_peer, cross_peer = (core_l, r, f), (far_l, r, f), (cross_l, r, f)

    pending = []

    def send(src, dst, ss, rs, peer):
        copy = pltpu.make_async_remote_copy(
            src_ref=src, dst_ref=dst, send_sem=ss, recv_sem=rs, device_id=peer, device_id_type=MESH
        )
        copy.start()
        pending.append(copy)

    def arrived(dst, ss, rs):
        pltpu.make_async_remote_copy(
            src_ref=dst, dst_ref=dst, send_sem=ss, recv_sem=rs, device_id=core_peer, device_id_type=MESH
        ).wait_recv()

    loads = [
        pltpu.make_async_copy(src, dst, load_sem.at[i])
        for i, (src, dst) in enumerate(
            ((resid, res_v), (down_w, dw), (enc_w, ew), (gate_w, gw), (up_w, uw), (dec_w, dv))
        )
    ]
    for copy in loads:
        copy.start()
    barrier = pltpu.get_barrier_semaphore()
    peers = [x_peer(d) for d in (1, 2, 3)] + [z_peer(d) for d in range(1, 8)]
    peers += [y_pair, core_peer, far_peer, cross_peer]
    for peer in peers:
        pl.semaphore_signal(barrier, inc=1, device_id=peer, device_id_type=MESH)

    loads[0].wait()

    def norm_rows(i, carry):
        rows = pl.ds(pl.multiple_of(i * 16, 16), 16)
        value = res_v[rows, :].astype(F32)
        inv = lax.rsqrt(jnp.mean(value * value, axis=-1, keepdims=True) + 1e-06)
        out = (value * inv * gain[...]).astype(BF16)
        xg[0, r, rows, :] = out[:, :1152]
        xg[1, r, rows, :] = out[:, 1152:]
        return carry

    lax.fori_loop(0, 8, norm_rows, 0)
    pl.semaphore_wait(barrier, len(peers))
    for d in (1, 3, 2):
        send(xg.at[half, r], xg.at[half, r], xa_ss.at[d - 1], xa_rs.at[d - 1], x_peer(d))

    loads[1].wait()
    for q in range(4):
        wsend[q] = dw[:, q * 576 : (q + 1) * 576]
    for i, (peer_l, peer) in enumerate(((core_l, core_peer), (far_l, far_peer), (cross_l, cross_peer))):
        send(wsend.at[peer_l], wd.at[l], w_ss.at[i], w_rs.at[i], peer)
    wd[l] = wsend[l]

    for copy in loads[2:5]:
        copy.wait()

    def features(chunk):
        left, right = xg[0, chunk], xg[1, chunk]
        pre = dot(left, ew[:1152]) + dot(right, ew[1152:]) + enc_b[...]
        fh[l, chunk, :, :512] = jnp.maximum(pre, 0.0).astype(BF16)
        gate = dot_t(left, gw[:, :1152]) + dot_t(right, gw[:, 1152:])
        up = dot_t(left, uw[:, :1152]) + dot_t(right, uw[:, 1152:])
        fh[l, chunk, :, 512:] = (gelu(gate) * up).astype(BF16)

    def share(d):
        chunk = (r - d) % 4
        features(chunk)
        send(fh.at[l, chunk], fh.at[l, chunk], fy_ss.at[d], fy_rs.at[d], far_peer)
        send(fh.at[l, chunk], fh.at[l, chunk], fc_ss.at[d], fc_rs.at[d], core_peer)

    def hand_on(d):
        chunk = (r - d) % 4
        arrived(fh.at[far_l, chunk], fy_ss.at[d], fy_rs.at[d])
        send(fh.at[far_l, chunk], fh.at[far_l, chunk], ff_ss.at[d], ff_rs.at[d], core_peer)

    def have(d):
        chunk = (r - d) % 4
        arrived(fh.at[core_l, chunk], fc_ss.at[d], fc_rs.at[d])
        arrived(fh.at[cross_l, chunk], ff_ss.at[d], ff_rs.at[d])

    low, high = pl.ds(0, 64), pl.ds(64, 64)

    def relay(d):
        chunk = (r - d) % 4
        arrived(xg.at[half, chunk], xa_ss.at[d - 1], xa_rs.at[d - 1])
        send(xg.at[half, chunk, low], xg.at[half, chunk, low], zf_ss.at[d - 1, 0], zf_rs.at[d - 1, 0], z_peer(1))
        send(xg.at[half, chunk, high], xg.at[half, chunk, high], zf_ss.at[d - 1, 1], zf_rs.at[d - 1, 1], z_peer(7))

    def rest(d):
        chunk = (r - d) % 4
        arrived(xg.at[other, chunk, low], zf_ss.at[d - 1, 0], zf_rs.at[d - 1, 0])
        arrived(xg.at[other, chunk, high], zf_ss.at[d - 1, 1], zf_rs.at[d - 1, 1])

    share(0)
    relay(1)
    relay(3)
    rest(1)
    share(1)
    relay(2)
    hand_on(0)
    rest(3)
    share(3)
    hand_on(1)
    rest(2)
    share(2)
    hand_on(3)
    hand_on(2)
    loads[5].wait()
    for i, peer_l in enumerate((core_l, far_l, cross_l)):
        arrived(wd.at[peer_l], w_ss.at[i], w_rs.at[i])
    for d in (0, 1, 3, 2):
        have(d)

    def partial_sum(t, chunk):
        total = -dot(fh[t, chunk, :, 512:], wd[t])
        for s in range(t + 1):
            total = total + dot_t(fh[s, chunk, :, :512], dv[pair_index(s, t)])
        return total

    def decode(t):
        for d in (2, 1, 3):
            chunk = (r + d) % 4
            xs[t, chunk] = partial_sum(t, chunk).astype(BF16)
            send(xs.at[t, chunk], xr.at[t, d - 1], x_ss.at[t, d - 1], x_rs.at[t, d - 1], x_peer(d))
        own[t] = partial_sum(t, r)

    def sum_x(t):
        for d in (1, 3, 2):
            arrived(xr.at[t, d - 1], x_ss.at[t, d - 1], x_rs.at[t, d - 1])

        def block(i, carry):
            rows = pl.ds(pl.multiple_of(i * 16, 16), 16)
            value = own[t, rows, :]
            for d in range(3):
                value = value + xr[t, d, rows, :].astype(F32)
            zf[t, i] = value
            zs[t, i] = value.astype(BF16)
            return carry

        lax.fori_loop(0, 8, block, 0)
        for d in (4, 3, 5, 2, 6, 1, 7):
            to = (z + d) % 8
            send(zs.at[t, to], zr.at[t, d - 1], z_ss.at[t, d - 1], z_rs.at[t, d - 1], z_peer(d))

    def sum_z(t):
        for d in range(1, 8):
            arrived(zr.at[t, d - 1], z_ss.at[t, d - 1], z_rs.at[t, d - 1])
        value = zf[t, z]
        for d in range(7):
            value = value + zr[t, d].astype(F32)
        ps[t] = value.astype(BF16)
        send(ps.at[t], pr.at[t], p_ss.at[t], p_rs.at[t], y_pair)

    def sum_pair(t):
        arrived(pr.at[t], p_ss.at[t], p_rs.at[t])
        value = ps[t].astype(F32) + pr[t].astype(F32) + dec_b[t : t + 1, :]
        ef[t] = value
        eg[t, r, z] = value.astype(BF16)
        err_out[t] = ef[t, pl.ds(pl.multiple_of(yl * 8, 8), 8), :].astype(BF16)
        for d in (4, 3, 5, 2, 6, 1, 7):
            send(eg.at[t, r, z], eg.at[t, r, z], az_ss.at[t, d - 1], az_rs.at[t, d - 1], z_peer(d))

    def gather_z(t):
        for d in range(1, 8):
            arrived(eg.at[t, r, (z - d) % 8], az_ss.at[t, d - 1], az_rs.at[t, d - 1])
        for d in (2, 1, 3):
            send(eg.at[t, r], eg.at[t, r], ax_ss.at[t, d - 1], ax_rs.at[t, d - 1], x_peer(d))

    def gradient(t):
        for d in (0, 1, 3, 2):
            chunk = (r - d) % 4
            if d:
                arrived(eg.at[t, chunk], ax_ss.at[t, d - 1], ax_rs.at[t, d - 1])
            errors = eg[t, chunk].reshape(128, 576)
            rows = pl.ds(pl.multiple_of(chunk * 128, 128), 128)
            for s in range(t, -1, -1):
                value = dot(errors, dv[pair_index(s, t)])
                if t < 3:
                    value = value + acc[s, rows, :]
                acc[s, rows, :] = value
                if s == t:
                    gs[s, rows, :] = value.astype(BF16)

    def core_send(s):
        @pl.when(c != s % 2)
        def _():
            pltpu.make_async_remote_copy(
                src_ref=gs.at[s], dst_ref=ga.at[s], send_sem=gc_ss.at[s], recv_sem=gc_rs.at[s],
                device_id=core_peer, device_id_type=MESH,
            ).start()

    def far_copy(s):
        return pltpu.make_async_remote_copy(
            src_ref=gt.at[s], dst_ref=gb, send_sem=gy_ss.at[s], recv_sem=gy_rs.at[s],
            device_id=far_peer, device_id_type=MESH,
        )

    def core_sum(s):
        @pl.when(c == s % 2)
        def _():
            arrived(ga.at[s], gc_ss.at[s], gc_rs.at[s])

            def block(i, carry):
                rows = pl.ds(pl.multiple_of(i * 32, 32), 32)
                value = acc[s, rows, :] + ga[s, rows, :].astype(F32)
                acc[s, rows, :] = value
                gt[s, rows, :] = value.astype(BF16)
                return carry

            lax.fori_loop(0, 16, block, 0)

            @pl.when(yh != s // 2)
            def _():
                far_copy(s).start()

    def finish(s):
        @pl.when(l == s)
        def _():
            far_copy(s).wait_recv()

            def block(i, carry):
                rows = pl.ds(pl.multiple_of(i * 32, 32), 32)
                act_out[rows, :] = (acc[s, rows, :] + gb[rows, :].astype(F32)).astype(BF16)
                return carry

            lax.fori_loop(0, 16, block, 0)

        @pl.when(c != s % 2)
        def _():
            pltpu.make_async_remote_copy(
                src_ref=gs.at[s], dst_ref=ga.at[s], send_sem=gc_ss.at[s], recv_sem=gc_rs.at[s],
                device_id=core_peer, device_id_type=MESH,
            ).wait_send()

        @pl.when((c == s % 2) & (yh != s // 2))
        def _():
            far_copy(s).wait_send()

    for t in (3, 2, 1, 0):
        decode(t)
    sum_x(3)
    sum_z(3)
    sum_pair(3)
    sum_x(2)
    gather_z(3)
    sum_z(2)
    sum_pair(2)
    sum_x(1)
    gather_z(2)
    sum_z(1)
    sum_pair(1)
    sum_x(0)
    gather_z(1)
    sum_z(0)
    sum_pair(0)
    gradient(3)
    core_send(3)
    gather_z(0)
    gradient(2)
    core_send(2)
    core_sum(3)
    gradient(1)
    core_send(1)
    core_sum(2)
    gradient(0)
    core_send(0)
    core_sum(1)
    core_sum(0)
    for s in (3, 2, 1, 0):
        finish(s)
    for copy in pending:
        copy.wait_send()


def body(resid, norm_gain, gate_weight, up_weight, down_weight, enc_weight, enc_bias, dec_weight, dec_bias):
    any_spec = pl.BlockSpec(memory_space=pl.ANY)
    vmem_spec = pl.BlockSpec(memory_space=pltpu.VMEM)
    vmem = pltpu.VMEM
    dma = pltpu.SemaphoreType.DMA
    scratch = [
        vmem((128, 2304), BF16),
        vmem((2, 4, 128, 1152), BF16),
        vmem((2304, 512), BF16),
        vmem((144, 2304), BF16),
        vmem((144, 2304), BF16),
        vmem((144, 2304), BF16),
        vmem((4, 144, 576), BF16),
        vmem((4, 144, 576), BF16),
        vmem((10, 576, 512), BF16),
        vmem((4, 4, 128, 656), BF16),
        vmem((4, 4, 128, 576), BF16),
        vmem((4, 128, 576), F32),
        vmem((4, 3, 128, 576), BF16),
        vmem((4, 8, 16, 576), F32),
        vmem((4, 8, 16, 576), BF16),
        vmem((4, 7, 16, 576), BF16),
        vmem((4, 16, 576), BF16),
        vmem((4, 16, 576), BF16),
        vmem((4, 16, 576), F32),
        vmem((4, 4, 8, 16, 576), BF16),
        vmem((4, 512, 512), F32),
        vmem((4, 512, 512), BF16),
        vmem((4, 512, 512), BF16),
        vmem((4, 512, 512), BF16),
        vmem((512, 512), BF16),
        dma((6,)),
    ]
    for shape in ((3,), (3,), (3, 2), (4,), (4,), (4,), (4, 3), (4, 7), (4,), (4, 7), (4, 3), (4,), (4,)):
        scratch += [dma(shape), dma(shape)]
    errors, act_grad = pl.pallas_call(
        kernel,
        out_shape=(
            jax.ShapeDtypeStruct((4, 8, 576), BF16),
            jax.ShapeDtypeStruct((512, 512), BF16),
        ),
        in_specs=[any_spec, vmem_spec, any_spec, any_spec, any_spec, any_spec, vmem_spec, any_spec, vmem_spec],
        out_specs=(vmem_spec, vmem_spec),
        scratch_shapes=scratch,
        compiler_params=pltpu.CompilerParams(
            collective_id=1, has_side_effects=True, vmem_limit_bytes=60 * 2**20
        ),
        cost_estimate=pl.CostEstimate(flops=8_200_000_000, bytes_accessed=12_000_000, transcendentals=100_000),
    )(
        resid[0], norm_gain, gate_weight[0], up_weight[0], down_weight[0], enc_weight[0], enc_bias,
        jnp.swapaxes(dec_weight, 1, 2), dec_bias,
    )
    return jnp.transpose(errors, (1, 0, 2)), act_grad[None]


def solution(mesh):
    in_specs = (
        P("layer", "rows", None),
        P("layer", None),
        P("layer", ("rows", "feat"), None),
        P("layer", ("rows", "feat"), None),
        P("layer", ("rows", "feat"), None),
        P("layer", None, ("rows", "feat")),
        P("layer", ("rows", "feat")),
        P(None, ("rows", "feat"), "layer"),
        P(None, "layer"),
    )
    out_specs = (P(("rows", "feat"), None, "layer"), P("layer", None, ("rows", "feat")))
    return jax.shard_map(body, mesh=mesh, in_specs=in_specs, out_specs=out_specs, check_vma=False)
```

```python
import jax
import jax.numpy as jnp
from jax import lax
from jax.experimental import pallas as pl
from jax.experimental.pallas import tpu as pltpu
from jax.sharding import PartitionSpec as P

MESH = pl.DeviceIdType.MESH
BF16 = jnp.bfloat16
F32 = jnp.float32
DIRECT_Z = (3, 0)
DIRECT_X = (0,)


def pair_index(source, target, layers=4):
    return source * layers - source * (source - 1) // 2 + target - source


def dot(left, right):
    return lax.dot_general(left, right, (((1,), (0,)), ((), ())), preferred_element_type=F32)


def dot_t(left, right):
    return lax.dot_general(left, right, (((1,), (1,)), ((), ())), preferred_element_type=F32)


def gelu(x):
    inner = 0.7978845608028654 * (x + 0.044715 * (x * x * x))
    return 0.5 * x * (1.0 + jnp.tanh(inner))


def kernel(
    resid, gain, gate_w, up_w, down_w, enc_w, enc_b, dec_w, dec_b,
    err_out, act_out,
    res_v, xg, ew, gw, uw, dw, wsend, wd, dv, fh,
    xs, own, xr, zf, zs, zr, ps, pr, ef, eg, acc, gs, ga, gt, gb,
    load_sem, w_ss, w_rs, xa_ss, xa_rs, xb_ss, xb_rs, zf_ss, zf_rs, fc_ss, fc_rs, fy_ss, fy_rs, ff_ss, ff_rs,
    x_ss, x_rs, z_ss, z_rs, p_ss, p_rs, az_ss, az_rs, ax_ss, ax_rs, ay_ss, ay_rs, gc_ss, gc_rs, gy_ss, gy_rs,
):
    l, r, f = lax.axis_index("layer"), lax.axis_index("rows"), lax.axis_index("feat")
    yh, c = l // 2, l % 2
    z, yl = f // 2, f % 2
    half = z % 2
    other = 1 - half

    def x_peer(d):
        return (l, (r + d) % 4, f)

    def z_peer(d):
        return (l, r, ((z + d) % 8) * 2 + yl)

    y_pair = (l, r, z * 2 + (1 - yl))
    core_l = yh * 2 + (1 - c)
    far_l = (1 - yh) * 2 + c
    cross_l = (1 - yh) * 2 + (1 - c)
    core_peer, far_peer, cross_peer = (core_l, r, f), (far_l, r, f), (cross_l, r, f)

    pending = []

    def send(src, dst, ss, rs, peer):
        copy = pltpu.make_async_remote_copy(
            src_ref=src, dst_ref=dst, send_sem=ss, recv_sem=rs, device_id=peer, device_id_type=MESH
        )
        copy.start()
        pending.append(copy)

    def arrived(dst, ss, rs):
        pltpu.make_async_remote_copy(
            src_ref=dst, dst_ref=dst, send_sem=ss, recv_sem=rs, device_id=core_peer, device_id_type=MESH
        ).wait_recv()

    loads = [
        pltpu.make_async_copy(src, dst, load_sem.at[i])
        for i, (src, dst) in enumerate(
            ((resid, res_v), (down_w, dw), (enc_w, ew), (gate_w, gw), (up_w, uw), (dec_w, dv))
        )
    ]
    for copy in loads:
        copy.start()
    barrier = pltpu.get_barrier_semaphore()
    peers = [x_peer(d) for d in (1, 2, 3)] + [z_peer(d) for d in range(1, 8)]
    peers += [y_pair, core_peer, far_peer, cross_peer]
    for peer in peers:
        pl.semaphore_signal(barrier, inc=1, device_id=peer, device_id_type=MESH)

    loads[0].wait()

    def norm_rows(i, carry):
        rows = pl.ds(pl.multiple_of(i * 16, 16), 16)
        value = res_v[rows, :].astype(F32)
        inv = lax.rsqrt(jnp.mean(value * value, axis=-1, keepdims=True) + 1e-06)
        out = (value * inv * gain[...]).astype(BF16)
        xg[0, r, rows, :] = out[:, :1152]
        xg[1, r, rows, :] = out[:, 1152:]
        return carry

    lax.fori_loop(0, 8, norm_rows, 0)
    pl.semaphore_wait(barrier, len(peers))
    for d in (1, 3):
        send(xg.at[half, r], xg.at[half, r], xa_ss.at[d - 1], xa_rs.at[d - 1], x_peer(d))

    loads[1].wait()
    for q in range(4):
        wsend[q] = dw[:, q * 576 : (q + 1) * 576]
    for i, (peer_l, peer) in enumerate(((core_l, core_peer), (far_l, far_peer), (cross_l, cross_peer))):
        send(wsend.at[peer_l], wd.at[l], w_ss.at[i], w_rs.at[i], peer)
    wd[l] = wsend[l]

    for copy in loads[2:5]:
        copy.wait()

    def features(chunk):
        left, right = xg[0, chunk], xg[1, chunk]
        pre = dot(left, ew[:1152]) + dot(right, ew[1152:]) + enc_b[...]
        fh[l, chunk, :, :512] = jnp.maximum(pre, 0.0).astype(BF16)
        gate = dot_t(left, gw[:, :1152]) + dot_t(right, gw[:, 1152:])
        up = dot_t(left, uw[:, :1152]) + dot_t(right, uw[:, 1152:])
        fh[l, chunk, :, 512:] = (gelu(gate) * up).astype(BF16)

    def share(d):
        chunk = (r - d) % 4
        features(chunk)
        send(fh.at[l, chunk], fh.at[l, chunk], fy_ss.at[d], fy_rs.at[d], far_peer)
        send(fh.at[l, chunk], fh.at[l, chunk], fc_ss.at[d], fc_rs.at[d], core_peer)

    def hand_on(d):
        chunk = (r - d) % 4
        arrived(fh.at[far_l, chunk], fy_ss.at[d], fy_rs.at[d])
        send(fh.at[far_l, chunk], fh.at[far_l, chunk], ff_ss.at[d], ff_rs.at[d], core_peer)

    def have(d):
        chunk = (r - d) % 4
        arrived(fh.at[core_l, chunk], fc_ss.at[d], fc_rs.at[d])
        arrived(fh.at[cross_l, chunk], ff_ss.at[d], ff_rs.at[d])

    low, high = pl.ds(0, 64), pl.ds(64, 64)

    def relay(d):
        chunk = (r - d) % 4
        parts = ((low, 1, 0, 1), (high, 3, 1, 7))
        if d != 2:
            arrived(xg.at[half, chunk], xa_ss.at[d - 1], xa_rs.at[d - 1])
            part, step, slot, _ = parts[d // 2]
            piece = xg.at[half, chunk, part]
            send(piece, piece, xb_ss.at[slot], xb_rs.at[slot], x_peer(step))
        for part, _, slot, z_step in parts:
            piece = xg.at[half, chunk, part]
            if d == 2:
                arrived(piece, xb_ss.at[slot], xb_rs.at[slot])
            send(piece, piece, zf_ss.at[d - 1, slot], zf_rs.at[d - 1, slot], z_peer(z_step))

    def rest(d):
        chunk = (r - d) % 4
        arrived(xg.at[other, chunk, low], zf_ss.at[d - 1, 0], zf_rs.at[d - 1, 0])
        arrived(xg.at[other, chunk, high], zf_ss.at[d - 1, 1], zf_rs.at[d - 1, 1])

    def partial_sum(t, chunk):
        total = -dot(fh[t, chunk, :, 512:], wd[t])
        for s in range(t + 1):
            total = total + dot_t(fh[s, chunk, :, :512], dv[pair_index(s, t)])
        return total

    def decode(d, targets):
        chunk = (r - d) % 4
        for t in targets:
            if d:
                xs[t, d - 1] = partial_sum(t, chunk).astype(BF16)
                send(xs.at[t, d - 1], xr.at[t, d - 1], x_ss.at[t, d - 1], x_rs.at[t, d - 1], x_peer(4 - d))
            else:
                own[t] = partial_sum(t, chunk)

    def sum_x(t):
        for d in (1, 3, 2):
            arrived(xr.at[t, d - 1], x_ss.at[t, d - 1], x_rs.at[t, d - 1])

        def block(i, carry):
            rows = pl.ds(pl.multiple_of(i * 16, 16), 16)
            value = own[t, rows, :]
            for d in range(3):
                value = value + xr[t, d, rows, :].astype(F32)
            zf[t, i] = value
            zs[t, i] = value.astype(BF16)
            return carry

        lax.fori_loop(0, 8, block, 0)
        for d in (4, 3, 5, 2, 6, 1, 7):
            to = (z + d) % 8
            send(zs.at[t, to], zr.at[t, d - 1], z_ss.at[t, d - 1], z_rs.at[t, d - 1], z_peer(d))

    def sum_z(t):
        for d in range(1, 8):
            arrived(zr.at[t, d - 1], z_ss.at[t, d - 1], z_rs.at[t, d - 1])
        value = zf[t, z]
        for d in range(7):
            value = value + zr[t, d].astype(F32)
        ps[t] = value.astype(BF16)
        send(ps.at[t], pr.at[t], p_ss.at[t], p_rs.at[t], y_pair)

    def send_z(t, origin, step, distance):
        piece = eg.at[t, r, (z - origin) % 8]
        send(piece, piece, az_ss.at[t, distance - 1], az_rs.at[t, distance - 1], z_peer(step))

    def arrived_z(t, d):
        arrived(eg.at[t, r, (z - d) % 8], az_ss.at[t, d - 1], az_rs.at[t, d - 1])

    def relay_z(t):
        arrived_z(t, 2)
        if t % 2 == 0:
            send_z(t, 2, 2, 4)
        send_z(t, 2, 1, 3)
        arrived_z(t, 6)
        if t % 2 == 1:
            send_z(t, 6, 6, 4)
        send_z(t, 6, 7, 5)

    def sum_pair(t):
        arrived(pr.at[t], p_ss.at[t], p_rs.at[t])
        value = ps[t].astype(F32) + pr[t].astype(F32) + dec_b[t : t + 1, :]
        ef[t] = value
        eg[t, r, z] = value.astype(BF16)
        err_out[t] = ef[t, pl.ds(pl.multiple_of(yl * 8, 8), 8), :].astype(BF16)
        for d in (4, 3, 5, 2, 6, 1, 7) if t in DIRECT_Z else (2, 6, 1, 7):
            send_z(t, 0, d, d)

    def gather_z(t):
        for d in (1, 2, 3, 4, 5, 6, 7) if t in DIRECT_Z else (1, 3, 4, 5, 7):
            arrived_z(t, d)
        for d in (2, 1, 3) if t in DIRECT_X else (1, 3):
            send(eg.at[t, r], eg.at[t, r], ax_ss.at[t, d - 1], ax_rs.at[t, d - 1], x_peer(d))

    first_z, last_z = pl.ds(0, 4), pl.ds(4, 4)

    def pass_on(t):
        for d, part, slot in ((1, first_z, 0), (3, last_z, 1)):
            chunk = (r - d) % 4
            arrived(eg.at[t, chunk], ax_ss.at[t, d - 1], ax_rs.at[t, d - 1])
            piece = eg.at[t, chunk, part]
            send(piece, piece, ay_ss.at[t, slot], ay_rs.at[t, slot], x_peer(d))

    def gradient(t, d):
        chunk = (r - d) % 4
        if d == 2:
            if t in DIRECT_X:
                arrived(eg.at[t, chunk], ax_ss.at[t, 1], ax_rs.at[t, 1])
            for part, slot in () if t in DIRECT_X else ((first_z, 0), (last_z, 1)):
                arrived(eg.at[t, chunk, part], ay_ss.at[t, slot], ay_rs.at[t, slot])
        elif d and t in DIRECT_X:
            arrived(eg.at[t, chunk], ax_ss.at[t, d - 1], ax_rs.at[t, d - 1])
        errors = eg[t, chunk].reshape(128, 576)
        for s in range(t, -1, -1):
            value = dot(errors, dv[pair_index(s, t)])
            if t < 3:
                value = value + acc[s, d]
            acc[s, d] = value
            if s == t:
                gs[s, d] = value.astype(BF16)

    def core_copy(s, d):
        return pltpu.make_async_remote_copy(
            src_ref=gs.at[s, d], dst_ref=ga.at[s, d], send_sem=gc_ss.at[s, d], recv_sem=gc_rs.at[s, d],
            device_id=core_peer, device_id_type=MESH,
        )

    def far_copy(s, d):
        return pltpu.make_async_remote_copy(
            src_ref=gt.at[s, d], dst_ref=gb.at[d], send_sem=gy_ss.at[s, d], recv_sem=gy_rs.at[s, d],
            device_id=far_peer, device_id_type=MESH,
        )

    def core_send(s, d):
        @pl.when(c != s % 2)
        def _():
            core_copy(s, d).start()

    def core_sum(s, d):
        @pl.when(c == s % 2)
        def _():
            core_copy(s, d).wait_recv()
            value = acc[s, d] + ga[s, d].astype(F32)
            acc[s, d] = value
            gt[s, d] = value.astype(BF16)

            @pl.when(yh != s // 2)
            def _():
                far_copy(s, d).start()

    def finish(s, d):
        @pl.when(l == s)
        def _():
            far_copy(s, d).wait_recv()
            rows = pl.ds(pl.multiple_of(((r - d) % 4) * 128, 128), 128)
            act_out[rows, :] = (acc[s, d] + gb[d].astype(F32)).astype(BF16)

        @pl.when(c != s % 2)
        def _():
            core_copy(s, d).wait_send()

        @pl.when((c == s % 2) & (yh != s // 2))
        def _():
            far_copy(s, d).wait_send()

    share(0)
    relay(1)
    relay(3)
    rest(1)
    share(1)
    hand_on(0)
    relay(2)
    rest(3)
    share(3)
    rest(2)
    share(2)
    hand_on(1)
    loads[5].wait()
    for i, peer_l in enumerate((core_l, far_l, cross_l)):
        arrived(wd.at[peer_l], w_ss.at[i], w_rs.at[i])
    have(0)
    decode(0, (3, 2))
    hand_on(3)
    have(1)
    decode(1, (3, 2))
    have(3)
    decode(3, (3, 2))
    hand_on(2)
    have(2)
    decode(2, (3, 2))
    decode(1, (1, 0))
    decode(3, (1, 0))
    decode(2, (1, 0))
    decode(0, (1, 0))
    sum_x(3)
    sum_x(2)
    sum_z(3)
    sum_pair(3)
    sum_z(2)
    sum_pair(2)
    gather_z(3)
    relay_z(2)
    sum_x(1)
    gather_z(2)
    sum_x(0)
    sum_z(1)
    sum_pair(1)
    pass_on(3)
    sum_z(0)
    relay_z(1)
    sum_pair(0)
    gather_z(1)
    pass_on(2)
    gather_z(0)
    order = (0, 1, 3, 2)

    def step(t, d):
        gradient(t, d)
        core_send(t, d)

    step(3, 0)
    step(3, 1)
    step(3, 3)
    pass_on(1)
    step(3, 2)
    step(2, 0)
    core_sum(3, 0)
    step(2, 1)
    core_sum(3, 1)
    step(2, 3)
    core_sum(3, 3)
    step(2, 2)
    core_sum(3, 2)
    for d in order:
        step(1, d)
        core_sum(2, d)
    for i, d in enumerate(order):
        step(0, d)
        core_sum(1, d)
        if i:
            core_sum(0, order[i - 1])
    core_sum(0, 2)
    for s in (3, 2, 1, 0):
        for d in order:
            finish(s, d)
    for copy in pending:
        copy.wait_send()


def write_out(errors, grads, err_out, act_out):
    err_out[...] = jnp.stack([errors[t].astype(F32) for t in range(4)], axis=1).astype(BF16)
    act_out[...] = grads[...]


def body(resid, norm_gain, gate_weight, up_weight, down_weight, enc_weight, enc_bias, dec_weight, dec_bias):
    any_spec = pl.BlockSpec(memory_space=pl.ANY)
    vmem_spec = pl.BlockSpec(memory_space=pltpu.VMEM)
    vmem = pltpu.VMEM
    dma = pltpu.SemaphoreType.DMA
    scratch = [
        vmem((128, 2304), BF16),
        vmem((2, 4, 128, 1152), BF16),
        vmem((2304, 512), BF16),
        vmem((144, 2304), BF16),
        vmem((144, 2304), BF16),
        vmem((144, 2304), BF16),
        vmem((4, 144, 576), BF16),
        vmem((4, 144, 576), BF16),
        vmem((10, 576, 512), BF16),
        vmem((4, 4, 128, 656), BF16),
        vmem((4, 3, 128, 576), BF16),
        vmem((4, 128, 576), F32),
        vmem((4, 3, 128, 576), BF16),
        vmem((4, 8, 16, 576), F32),
        vmem((4, 8, 16, 576), BF16),
        vmem((4, 7, 16, 576), BF16),
        vmem((4, 16, 576), BF16),
        vmem((4, 16, 576), BF16),
        vmem((4, 16, 576), F32),
        vmem((4, 4, 8, 16, 576), BF16),
        vmem((4, 4, 128, 512), F32),
        vmem((4, 4, 128, 512), BF16),
        vmem((4, 4, 128, 512), BF16),
        vmem((4, 4, 128, 512), BF16),
        vmem((4, 128, 512), BF16),
        dma((6,)),
    ]
    for shape in ((3,), (3,), (2,), (3, 2), (4,), (4,), (4,), (4, 3), (4, 7), (4,), (4, 7), (4, 3), (4, 2), (4, 4), (4, 4)):
        scratch += [dma(shape), dma(shape)]
    errors, act_grad = pl.pallas_call(
        kernel,
        out_shape=(
            jax.ShapeDtypeStruct((4, 8, 576), BF16),
            jax.ShapeDtypeStruct((512, 512), BF16),
        ),
        in_specs=[any_spec, vmem_spec, any_spec, any_spec, any_spec, any_spec, vmem_spec, any_spec, vmem_spec],
        out_specs=(vmem_spec, vmem_spec),
        scratch_shapes=scratch,
        compiler_params=pltpu.CompilerParams(
            collective_id=1, has_side_effects=True, vmem_limit_bytes=60 * 2**20
        ),
        cost_estimate=pl.CostEstimate(flops=8_200_000_000, bytes_accessed=12_000_000, transcendentals=100_000),
    )(
        resid[0], norm_gain, gate_weight[0], up_weight[0], down_weight[0], enc_weight[0], enc_bias,
        jnp.swapaxes(dec_weight, 1, 2), dec_bias,
    )
    return pl.pallas_call(
        write_out,
        out_shape=(jax.ShapeDtypeStruct((8, 4, 576), BF16), jax.ShapeDtypeStruct((1, 512, 512), BF16)),
        in_specs=[vmem_spec, vmem_spec],
        out_specs=(vmem_spec, vmem_spec),
    )(errors, act_grad[None])


def solution(mesh):
    in_specs = (
        P("layer", "rows", None),
        P("layer", None),
        P("layer", ("rows", "feat"), None),
        P("layer", ("rows", "feat"), None),
        P("layer", ("rows", "feat"), None),
        P("layer", None, ("rows", "feat")),
        P("layer", ("rows", "feat")),
        P(None, ("rows", "feat"), "layer"),
        P(None, "layer"),
    )
    out_specs = (P(("rows", "feat"), None, "layer"), P("layer", None, ("rows", "feat")))
    return jax.shard_map(body, mesh=mesh, in_specs=in_specs, out_specs=out_specs, check_vma=False)
```

```python
import jax
import jax.numpy as jnp
from jax import lax
from jax.experimental import pallas as pl
from jax.experimental.pallas import tpu as pltpu
from jax.sharding import PartitionSpec as P

MESH = pl.DeviceIdType.MESH
BF16 = jnp.bfloat16
F32 = jnp.float32
DIRECT_Z = (3, 2, 1, 0)
DIRECT_X = (0,)


def pair_index(source, target, layers=4):
    return source * layers - source * (source - 1) // 2 + target - source


def dot(left, right):
    return lax.dot_general(left, right, (((1,), (0,)), ((), ())), preferred_element_type=F32)


def dot_t(left, right):
    return lax.dot_general(left, right, (((1,), (1,)), ((), ())), preferred_element_type=F32)


def gelu(x):
    inner = 0.7978845608028654 * (x + 0.044715 * (x * x * x))
    return 0.5 * x * (1.0 + jnp.tanh(inner))


def kernel(
    resid, gain, gate_w, up_w, down_w, enc_w, enc_b, dec_w, dec_b,
    err_out, act_out,
    res_v, xg, ew, gw, uw, dw, wsend, wd, dv, fh,
    xs, own, xr, zf, zs, zr, ps, pr, ef, eg, acc, gs, ga, gt, gb,
    load_sem, w_ss, w_rs, xa_ss, xa_rs, xb_ss, xb_rs, zf_ss, zf_rs, fc_ss, fc_rs, fy_ss, fy_rs, ff_ss, ff_rs,
    x_ss, x_rs, z_ss, z_rs, p_ss, p_rs, az_ss, az_rs, ax_ss, ax_rs, ay_ss, ay_rs, gc_ss, gc_rs, gy_ss, gy_rs,
    hh, hy_ss, hy_rs, hc_ss, hc_rs, hf_ss, hf_rs,
):
    l, r, f = lax.axis_index("layer"), lax.axis_index("rows"), lax.axis_index("feat")
    yh, c = l // 2, l % 2
    z, yl = f // 2, f % 2
    half = z % 2
    other = 1 - half

    def x_peer(d):
        return (l, (r + d) % 4, f)

    def z_peer(d):
        return (l, r, ((z + d) % 8) * 2 + yl)

    y_pair = (l, r, z * 2 + (1 - yl))
    core_l = yh * 2 + (1 - c)
    far_l = (1 - yh) * 2 + c
    cross_l = (1 - yh) * 2 + (1 - c)
    core_peer, far_peer, cross_peer = (core_l, r, f), (far_l, r, f), (cross_l, r, f)

    pending = []

    def send(src, dst, ss, rs, peer):
        copy = pltpu.make_async_remote_copy(
            src_ref=src, dst_ref=dst, send_sem=ss, recv_sem=rs, device_id=peer, device_id_type=MESH
        )
        copy.start()
        pending.append(copy)

    def arrived(dst, ss, rs):
        pltpu.make_async_remote_copy(
            src_ref=dst, dst_ref=dst, send_sem=ss, recv_sem=rs, device_id=core_peer, device_id_type=MESH
        ).wait_recv()

    loads = [
        pltpu.make_async_copy(src, dst, load_sem.at[i])
        for i, (src, dst) in enumerate(
            ((resid, res_v), (down_w, dw), (enc_w, ew), (gate_w, gw), (up_w, uw), (dec_w, dv))
        )
    ]
    for copy in loads:
        copy.start()
    barrier = pltpu.get_barrier_semaphore()
    peers = [x_peer(d) for d in (1, 2, 3)] + [z_peer(d) for d in range(1, 8)]
    peers += [y_pair, core_peer, far_peer, cross_peer]
    for peer in peers:
        pl.semaphore_signal(barrier, inc=1, device_id=peer, device_id_type=MESH)

    loads[0].wait()

    def norm_rows(i, carry):
        rows = pl.ds(pl.multiple_of(i * 16, 16), 16)
        value = res_v[rows, :].astype(F32)
        inv = lax.rsqrt(jnp.mean(value * value, axis=-1, keepdims=True) + 1e-06)
        out = (value * inv * gain[...]).astype(BF16)
        xg[0, r, rows, :] = out[:, :1152]
        xg[1, r, rows, :] = out[:, 1152:]
        return carry

    lax.fori_loop(0, 8, norm_rows, 0)
    pl.semaphore_wait(barrier, len(peers))
    for d in (1, 3):
        send(xg.at[half, r], xg.at[half, r], xa_ss.at[d - 1], xa_rs.at[d - 1], x_peer(d))

    loads[1].wait()
    for q in range(4):
        wsend[q] = dw[:, q * 576 : (q + 1) * 576]
    for i, (peer_l, peer) in enumerate(((core_l, core_peer), (far_l, far_peer), (cross_l, cross_peer))):
        send(wsend.at[peer_l], wd.at[l], w_ss.at[i], w_rs.at[i], peer)
    wd[l] = wsend[l]

    for copy in loads[2:5]:
        copy.wait()

    def features(chunk):
        left, right = xg[0, chunk], xg[1, chunk]
        pre = dot(left, ew[:1152]) + dot(right, ew[1152:]) + enc_b[...]
        fh[l, chunk] = jnp.maximum(pre, 0.0).astype(BF16)
        gate = dot_t(gw[:, :1152], left) + dot_t(gw[:, 1152:], right)
        up = dot_t(uw[:, :1152], left) + dot_t(uw[:, 1152:], right)
        hh[l, chunk] = (gelu(gate) * up).astype(BF16)

    def share(d):
        chunk = (r - d) % 4
        features(chunk)
        send(fh.at[l, chunk], fh.at[l, chunk], fy_ss.at[d], fy_rs.at[d], far_peer)
        send(hh.at[l, chunk], hh.at[l, chunk], hy_ss.at[d], hy_rs.at[d], far_peer)
        send(fh.at[l, chunk], fh.at[l, chunk], fc_ss.at[d], fc_rs.at[d], core_peer)
        send(hh.at[l, chunk], hh.at[l, chunk], hc_ss.at[d], hc_rs.at[d], core_peer)

    def hand_on(d):
        chunk = (r - d) % 4
        arrived(fh.at[far_l, chunk], fy_ss.at[d], fy_rs.at[d])
        arrived(hh.at[far_l, chunk], hy_ss.at[d], hy_rs.at[d])
        send(fh.at[far_l, chunk], fh.at[far_l, chunk], ff_ss.at[d], ff_rs.at[d], core_peer)
        send(hh.at[far_l, chunk], hh.at[far_l, chunk], hf_ss.at[d], hf_rs.at[d], core_peer)

    def have(d):
        chunk = (r - d) % 4
        arrived(fh.at[core_l, chunk], fc_ss.at[d], fc_rs.at[d])
        arrived(hh.at[core_l, chunk], hc_ss.at[d], hc_rs.at[d])
        arrived(fh.at[cross_l, chunk], ff_ss.at[d], ff_rs.at[d])
        arrived(hh.at[cross_l, chunk], hf_ss.at[d], hf_rs.at[d])

    low, high = pl.ds(0, 64), pl.ds(64, 64)

    def relay(d):
        chunk = (r - d) % 4
        parts = ((low, 1, 0, 1), (high, 3, 1, 7))
        if d != 2:
            arrived(xg.at[half, chunk], xa_ss.at[d - 1], xa_rs.at[d - 1])
            part, step, slot, _ = parts[d // 2]
            piece = xg.at[half, chunk, part]
            send(piece, piece, xb_ss.at[slot], xb_rs.at[slot], x_peer(step))
        for part, _, slot, z_step in parts:
            piece = xg.at[half, chunk, part]
            if d == 2:
                arrived(piece, xb_ss.at[slot], xb_rs.at[slot])
            send(piece, piece, zf_ss.at[d - 1, slot], zf_rs.at[d - 1, slot], z_peer(z_step))

    def rest(d):
        chunk = (r - d) % 4
        arrived(xg.at[other, chunk, low], zf_ss.at[d - 1, 0], zf_rs.at[d - 1, 0])
        arrived(xg.at[other, chunk, high], zf_ss.at[d - 1, 1], zf_rs.at[d - 1, 1])

    def partial_sum(t, chunk):
        total = -lax.dot_general(
            hh[t, chunk], wd[t], (((0,), (0,)), ((), ())), preferred_element_type=F32
        )
        for s in range(t + 1):
            total = total + dot_t(fh[s, chunk], dv[pair_index(s, t)])
        return total

    def decode(d, targets):
        chunk = (r - d) % 4
        for t in targets:
            if d:
                xs[t, d - 1] = partial_sum(t, chunk).astype(BF16)
                send(xs.at[t, d - 1], xr.at[t, d - 1], x_ss.at[t, d - 1], x_rs.at[t, d - 1], x_peer(4 - d))
            else:
                own[t] = partial_sum(t, chunk)

    def sum_x(t):
        for d in (1, 3, 2):
            arrived(xr.at[t, d - 1], x_ss.at[t, d - 1], x_rs.at[t, d - 1])

        def block(i, carry):
            rows = pl.ds(pl.multiple_of(i * 16, 16), 16)
            value = own[t, rows, :]
            for d in range(3):
                value = value + xr[t, d, rows, :].astype(F32)
            zf[t, i] = value
            zs[t, i] = value.astype(BF16)
            return carry

        lax.fori_loop(0, 8, block, 0)
        for d in (4, 3, 5, 2, 6, 1, 7):
            to = (z + d) % 8
            send(zs.at[t, to], zr.at[t, d - 1], z_ss.at[t, d - 1], z_rs.at[t, d - 1], z_peer(d))

    def sum_z(t):
        for d in range(1, 8):
            arrived(zr.at[t, d - 1], z_ss.at[t, d - 1], z_rs.at[t, d - 1])
        value = zf[t, z]
        for d in range(7):
            value = value + zr[t, d].astype(F32)
        ps[t] = value.astype(BF16)
        send(ps.at[t], pr.at[t], p_ss.at[t], p_rs.at[t], y_pair)

    def send_z(t, origin, step, distance):
        piece = eg.at[t, r, (z - origin) % 8]
        send(piece, piece, az_ss.at[t, distance - 1], az_rs.at[t, distance - 1], z_peer(step))

    def arrived_z(t, d):
        arrived(eg.at[t, r, (z - d) % 8], az_ss.at[t, d - 1], az_rs.at[t, d - 1])

    def relay_z(t):
        arrived_z(t, 2)
        if t % 2 == 0:
            send_z(t, 2, 2, 4)
        send_z(t, 2, 1, 3)
        arrived_z(t, 6)
        if t % 2 == 1:
            send_z(t, 6, 6, 4)
        send_z(t, 6, 7, 5)

    def sum_pair(t):
        arrived(pr.at[t], p_ss.at[t], p_rs.at[t])
        value = ps[t].astype(F32) + pr[t].astype(F32) + dec_b[t : t + 1, :]
        ef[t] = value
        eg[t, r, z] = value.astype(BF16)
        err_out[t] = ef[t, pl.ds(pl.multiple_of(yl * 8, 8), 8), :].astype(BF16)
        for d in (4, 3, 5, 2, 6, 1, 7) if t in DIRECT_Z else (2, 6, 1, 7):
            send_z(t, 0, d, d)

    def gather_z(t):
        for d in (1, 2, 3, 4, 5, 6, 7) if t in DIRECT_Z else (1, 3, 4, 5, 7):
            arrived_z(t, d)
        for d in (2, 1, 3) if t in DIRECT_X else (1, 3):
            send(eg.at[t, r], eg.at[t, r], ax_ss.at[t, d - 1], ax_rs.at[t, d - 1], x_peer(d))

    first_z, last_z = pl.ds(0, 4), pl.ds(4, 4)

    def pass_on(t):
        for d, part, slot in ((1, first_z, 0), (3, last_z, 1)):
            chunk = (r - d) % 4
            arrived(eg.at[t, chunk], ax_ss.at[t, d - 1], ax_rs.at[t, d - 1])
            piece = eg.at[t, chunk, part]
            send(piece, piece, ay_ss.at[t, slot], ay_rs.at[t, slot], x_peer(d))

    def gradient(t, d):
        chunk = (r - d) % 4
        if d == 2:
            if t in DIRECT_X:
                arrived(eg.at[t, chunk], ax_ss.at[t, 1], ax_rs.at[t, 1])
            for part, slot in () if t in DIRECT_X else ((first_z, 0), (last_z, 1)):
                arrived(eg.at[t, chunk, part], ay_ss.at[t, slot], ay_rs.at[t, slot])
        elif d and t in DIRECT_X:
            arrived(eg.at[t, chunk], ax_ss.at[t, d - 1], ax_rs.at[t, d - 1])
        errors = eg[t, chunk].reshape(128, 576)
        for s in range(t, -1, -1):
            value = dot(errors, dv[pair_index(s, t)])
            if t < 3:
                value = value + acc[s, d]
            acc[s, d] = value
            if s == t:
                gs[s, d] = value.astype(BF16)

    def core_copy(s, d):
        return pltpu.make_async_remote_copy(
            src_ref=gs.at[s, d], dst_ref=ga.at[s, d], send_sem=gc_ss.at[s, d], recv_sem=gc_rs.at[s, d],
            device_id=core_peer, device_id_type=MESH,
        )

    def far_copy(s, d):
        return pltpu.make_async_remote_copy(
            src_ref=gt.at[s, d], dst_ref=gb.at[d], send_sem=gy_ss.at[s, d], recv_sem=gy_rs.at[s, d],
            device_id=far_peer, device_id_type=MESH,
        )

    def core_send(s, d):
        @pl.when(c != s % 2)
        def _():
            core_copy(s, d).start()

    def core_sum(s, d):
        @pl.when(c == s % 2)
        def _():
            core_copy(s, d).wait_recv()
            value = acc[s, d] + ga[s, d].astype(F32)
            acc[s, d] = value
            gt[s, d] = value.astype(BF16)

            @pl.when(yh != s // 2)
            def _():
                far_copy(s, d).start()

    def finish(s, d):
        @pl.when(l == s)
        def _():
            far_copy(s, d).wait_recv()
            rows = pl.ds(pl.multiple_of(((r - d) % 4) * 128, 128), 128)
            act_out[rows, :] = (acc[s, d] + gb[d].astype(F32)).astype(BF16)

        @pl.when(c != s % 2)
        def _():
            core_copy(s, d).wait_send()

        @pl.when((c == s % 2) & (yh != s // 2))
        def _():
            far_copy(s, d).wait_send()

    share(0)
    relay(1)
    relay(3)
    rest(1)
    share(1)
    hand_on(0)
    relay(2)
    rest(3)
    share(3)
    rest(2)
    share(2)
    hand_on(1)
    loads[5].wait()
    for i, peer_l in enumerate((core_l, far_l, cross_l)):
        arrived(wd.at[peer_l], w_ss.at[i], w_rs.at[i])
    have(0)
    decode(0, (3, 2))
    hand_on(3)
    have(1)
    decode(1, (3, 2))
    have(3)
    decode(3, (3, 2))
    hand_on(2)
    have(2)
    decode(2, (3, 2))
    decode(1, (1, 0))
    decode(3, (1, 0))
    decode(2, (1, 0))
    decode(0, (1, 0))
    sum_x(3)
    sum_x(2)
    sum_z(3)
    sum_pair(3)
    sum_z(2)
    sum_pair(2)
    gather_z(3)
    sum_x(1)
    gather_z(2)
    sum_x(0)
    sum_z(1)
    sum_pair(1)
    pass_on(3)
    sum_z(0)
    sum_pair(0)
    gather_z(1)
    pass_on(2)
    gather_z(0)
    order = (0, 1, 3, 2)

    def step(t, d):
        gradient(t, d)
        core_send(t, d)

    step(3, 0)
    step(3, 1)
    step(3, 3)
    pass_on(1)
    step(3, 2)
    step(2, 0)
    core_sum(3, 0)
    step(2, 1)
    core_sum(3, 1)
    step(2, 3)
    core_sum(3, 3)
    step(2, 2)
    core_sum(3, 2)
    for d in order:
        step(1, d)
        core_sum(2, d)
    for i, d in enumerate(order):
        step(0, d)
        core_sum(1, d)
        if i:
            core_sum(0, order[i - 1])
    core_sum(0, 2)
    for s in (3, 2, 1, 0):
        for d in order:
            finish(s, d)
    for copy in pending:
        copy.wait_send()


def write_out(errors, grads, err_out, act_out):
    err_out[...] = jnp.stack([errors[t].astype(F32) for t in range(4)], axis=1).astype(BF16)
    act_out[...] = grads[...]


def body(resid, norm_gain, gate_weight, up_weight, down_weight, enc_weight, enc_bias, dec_weight, dec_bias):
    any_spec = pl.BlockSpec(memory_space=pl.ANY)
    vmem_spec = pl.BlockSpec(memory_space=pltpu.VMEM)
    vmem = pltpu.VMEM
    dma = pltpu.SemaphoreType.DMA
    scratch = [
        vmem((128, 2304), BF16),
        vmem((2, 4, 128, 1152), BF16),
        vmem((2304, 512), BF16),
        vmem((144, 2304), BF16),
        vmem((144, 2304), BF16),
        vmem((144, 2304), BF16),
        vmem((4, 144, 576), BF16),
        vmem((4, 144, 576), BF16),
        vmem((10, 576, 512), BF16),
        vmem((4, 4, 128, 512), BF16),
        vmem((4, 3, 128, 576), BF16),
        vmem((4, 128, 576), F32),
        vmem((4, 3, 128, 576), BF16),
        vmem((4, 8, 16, 576), F32),
        vmem((4, 8, 16, 576), BF16),
        vmem((4, 7, 16, 576), BF16),
        vmem((4, 16, 576), BF16),
        vmem((4, 16, 576), BF16),
        vmem((4, 16, 576), F32),
        vmem((4, 4, 8, 16, 576), BF16),
        vmem((4, 4, 128, 512), F32),
        vmem((4, 4, 128, 512), BF16),
        vmem((4, 4, 128, 512), BF16),
        vmem((4, 4, 128, 512), BF16),
        vmem((4, 128, 512), BF16),
        dma((6,)),
    ]
    for shape in ((3,), (3,), (2,), (3, 2), (4,), (4,), (4,), (4, 3), (4, 7), (4,), (4, 7), (4, 3), (4, 2), (4, 4), (4, 4)):
        scratch += [dma(shape), dma(shape)]
    scratch += [vmem((4, 4, 144, 128), BF16)] + [dma((4,)) for _ in range(6)]
    errors, act_grad = pl.pallas_call(
        kernel,
        out_shape=(
            jax.ShapeDtypeStruct((4, 8, 576), BF16),
            jax.ShapeDtypeStruct((512, 512), BF16),
        ),
        in_specs=[any_spec, vmem_spec, any_spec, any_spec, any_spec, any_spec, vmem_spec, any_spec, vmem_spec],
        out_specs=(vmem_spec, vmem_spec),
        scratch_shapes=scratch,
        compiler_params=pltpu.CompilerParams(
            collective_id=1, has_side_effects=True, vmem_limit_bytes=60 * 2**20
        ),
        cost_estimate=pl.CostEstimate(flops=8_200_000_000, bytes_accessed=12_000_000, transcendentals=100_000),
    )(
        resid[0], norm_gain, gate_weight[0], up_weight[0], down_weight[0], enc_weight[0], enc_bias,
        jnp.swapaxes(dec_weight, 1, 2), dec_bias,
    )
    return pl.pallas_call(
        write_out,
        out_shape=(jax.ShapeDtypeStruct((8, 4, 576), BF16), jax.ShapeDtypeStruct((1, 512, 512), BF16)),
        in_specs=[vmem_spec, vmem_spec],
        out_specs=(vmem_spec, vmem_spec),
    )(errors, act_grad[None])


def solution(mesh):
    in_specs = (
        P("layer", "rows", None),
        P("layer", None),
        P("layer", ("rows", "feat"), None),
        P("layer", ("rows", "feat"), None),
        P("layer", ("rows", "feat"), None),
        P("layer", None, ("rows", "feat")),
        P("layer", ("rows", "feat")),
        P(None, ("rows", "feat"), "layer"),
        P(None, "layer"),
    )
    out_specs = (P(("rows", "feat"), None, "layer"), P("layer", None, ("rows", "feat")))
    return jax.shard_map(body, mesh=mesh, in_specs=in_specs, out_specs=out_specs, check_vma=False)
```

```python
import jax
import jax.numpy as jnp
from jax import lax
from jax.experimental import pallas as pl
from jax.experimental.pallas import tpu as pltpu
from jax.sharding import PartitionSpec as P

MESH = pl.DeviceIdType.MESH
BF16 = jnp.bfloat16
F32 = jnp.float32
DIRECT_Z = (3, 2, 1, 0)
DIRECT_X = (1, 0)


def pair_index(source, target, layers=4):
    return source * layers - source * (source - 1) // 2 + target - source


def dot(left, right):
    return lax.dot_general(left, right, (((1,), (0,)), ((), ())), preferred_element_type=F32)


def dot_t(left, right):
    return lax.dot_general(left, right, (((1,), (1,)), ((), ())), preferred_element_type=F32)


def gelu(x):
    inner = 0.7978845608028654 * (x + 0.044715 * (x * x * x))
    return 0.5 * x * (1.0 + jnp.tanh(inner))


def kernel(
    resid, gain, gate_w, up_w, down_w, enc_w, enc_b, dec_w, dec_b,
    err_out, act_out,
    res_v, xg, ew, gw, uw, dw, wsend, wd, dv, fh,
    xs, own, xr, zf, zs, zr, ps, pr, ef, eg, acc, gs, ga, gt, gb,
    load_sem, w_ss, w_rs, xa_ss, xa_rs, xb_ss, xb_rs, zf_ss, zf_rs, fc_ss, fc_rs, fy_ss, fy_rs, ff_ss, ff_rs,
    x_ss, x_rs, z_ss, z_rs, p_ss, p_rs, az_ss, az_rs, ax_ss, ax_rs, ay_ss, ay_rs, gc_ss, gc_rs, gy_ss, gy_rs,
    hh, hy_ss, hy_rs, hc_ss, hc_rs, hf_ss, hf_rs,
):
    l, r, f = lax.axis_index("layer"), lax.axis_index("rows"), lax.axis_index("feat")
    yh, c = l // 2, l % 2
    z, yl = f // 2, f % 2
    half = z % 2
    other = 1 - half

    def x_peer(d):
        return (l, (r + d) % 4, f)

    def z_peer(d):
        return (l, r, ((z + d) % 8) * 2 + yl)

    y_pair = (l, r, z * 2 + (1 - yl))
    core_l = yh * 2 + (1 - c)
    far_l = (1 - yh) * 2 + c
    cross_l = (1 - yh) * 2 + (1 - c)
    core_peer, far_peer, cross_peer = (core_l, r, f), (far_l, r, f), (cross_l, r, f)

    pending = []

    def send(src, dst, ss, rs, peer):
        copy = pltpu.make_async_remote_copy(
            src_ref=src, dst_ref=dst, send_sem=ss, recv_sem=rs, device_id=peer, device_id_type=MESH
        )
        copy.start()
        pending.append(copy)

    def arrived(dst, ss, rs):
        pltpu.make_async_remote_copy(
            src_ref=dst, dst_ref=dst, send_sem=ss, recv_sem=rs, device_id=core_peer, device_id_type=MESH
        ).wait_recv()

    loads = [
        pltpu.make_async_copy(src, dst, load_sem.at[i])
        for i, (src, dst) in enumerate(
            ((resid, res_v), (down_w, dw), (enc_w, ew), (gate_w, gw), (up_w, uw), (dec_w, dv))
        )
    ]
    for copy in loads:
        copy.start()
    barrier = pltpu.get_barrier_semaphore()
    peers = [x_peer(d) for d in (1, 2, 3)] + [z_peer(d) for d in range(1, 8)]
    peers += [y_pair, core_peer, far_peer, cross_peer]
    for peer in peers:
        pl.semaphore_signal(barrier, inc=1, device_id=peer, device_id_type=MESH)

    loads[0].wait()

    def norm_rows(i, carry):
        rows = pl.ds(pl.multiple_of(i * 16, 16), 16)
        value = res_v[rows, :].astype(F32)
        inv = lax.rsqrt(jnp.mean(value * value, axis=-1, keepdims=True) + 1e-06)
        out = (value * inv * gain[...]).astype(BF16)
        xg[0, r, rows, :] = out[:, :1152]
        xg[1, r, rows, :] = out[:, 1152:]
        return carry

    lax.fori_loop(0, 8, norm_rows, 0)
    pl.semaphore_wait(barrier, len(peers))
    for d in (1, 3):
        send(xg.at[half, r], xg.at[half, r], xa_ss.at[d - 1], xa_rs.at[d - 1], x_peer(d))

    loads[1].wait()
    for q in range(4):
        wsend[q] = dw[:, q * 576 : (q + 1) * 576]
    for i, (peer_l, peer) in enumerate(((core_l, core_peer), (far_l, far_peer), (cross_l, cross_peer))):
        send(wsend.at[peer_l], wd.at[l], w_ss.at[i], w_rs.at[i], peer)
    wd[l] = wsend[l]

    for copy in loads[2:5]:
        copy.wait()

    def features(chunk):
        left, right = xg[0, chunk], xg[1, chunk]
        pre = dot(left, ew[:1152]) + dot(right, ew[1152:]) + enc_b[...]
        fh[l, chunk] = jnp.maximum(pre, 0.0).astype(BF16)
        gate = dot_t(gw[:, :1152], left) + dot_t(gw[:, 1152:], right)
        up = dot_t(uw[:, :1152], left) + dot_t(uw[:, 1152:], right)
        hh[l, chunk] = (gelu(gate) * up).astype(BF16)

    def share(d):
        chunk = (r - d) % 4
        features(chunk)
        send(fh.at[l, chunk], fh.at[l, chunk], fy_ss.at[d], fy_rs.at[d], far_peer)
        send(hh.at[l, chunk], hh.at[l, chunk], hy_ss.at[d], hy_rs.at[d], far_peer)
        send(fh.at[l, chunk], fh.at[l, chunk], fc_ss.at[d], fc_rs.at[d], core_peer)
        send(hh.at[l, chunk], hh.at[l, chunk], hc_ss.at[d], hc_rs.at[d], core_peer)

    def hand_on(d):
        chunk = (r - d) % 4
        arrived(fh.at[far_l, chunk], fy_ss.at[d], fy_rs.at[d])
        arrived(hh.at[far_l, chunk], hy_ss.at[d], hy_rs.at[d])
        send(fh.at[far_l, chunk], fh.at[far_l, chunk], ff_ss.at[d], ff_rs.at[d], core_peer)
        send(hh.at[far_l, chunk], hh.at[far_l, chunk], hf_ss.at[d], hf_rs.at[d], core_peer)

    def have(d):
        chunk = (r - d) % 4
        arrived(fh.at[core_l, chunk], fc_ss.at[d], fc_rs.at[d])
        arrived(hh.at[core_l, chunk], hc_ss.at[d], hc_rs.at[d])
        arrived(fh.at[cross_l, chunk], ff_ss.at[d], ff_rs.at[d])
        arrived(hh.at[cross_l, chunk], hf_ss.at[d], hf_rs.at[d])

    low, high = pl.ds(0, 64), pl.ds(64, 64)

    def relay(d):
        chunk = (r - d) % 4
        parts = ((low, 1, 0, 1), (high, 3, 1, 7))
        if d != 2:
            arrived(xg.at[half, chunk], xa_ss.at[d - 1], xa_rs.at[d - 1])
            part, step, slot, _ = parts[d // 2]
            piece = xg.at[half, chunk, part]
            send(piece, piece, xb_ss.at[slot], xb_rs.at[slot], x_peer(step))
        for part, _, slot, z_step in parts:
            piece = xg.at[half, chunk, part]
            if d == 2:
                arrived(piece, xb_ss.at[slot], xb_rs.at[slot])
            send(piece, piece, zf_ss.at[d - 1, slot], zf_rs.at[d - 1, slot], z_peer(z_step))

    def rest(d):
        chunk = (r - d) % 4
        arrived(xg.at[other, chunk, low], zf_ss.at[d - 1, 0], zf_rs.at[d - 1, 0])
        arrived(xg.at[other, chunk, high], zf_ss.at[d - 1, 1], zf_rs.at[d - 1, 1])

    def partial_sum(t, chunk):
        total = -lax.dot_general(
            hh[t, chunk], wd[t], (((0,), (0,)), ((), ())), preferred_element_type=F32
        )
        for s in range(t + 1):
            total = total + dot_t(fh[s, chunk], dv[pair_index(s, t)])
        return total

    def decode(d, targets):
        chunk = (r - d) % 4
        for t in targets:
            if d:
                xs[t, d - 1] = partial_sum(t, chunk).astype(BF16)
                send(xs.at[t, d - 1], xr.at[t, d - 1], x_ss.at[t, d - 1], x_rs.at[t, d - 1], x_peer(4 - d))
            else:
                own[t] = partial_sum(t, chunk)

    def sum_x(t):
        for d in (1, 3, 2):
            arrived(xr.at[t, d - 1], x_ss.at[t, d - 1], x_rs.at[t, d - 1])

        def block(i, carry):
            rows = pl.ds(pl.multiple_of(i * 16, 16), 16)
            value = own[t, rows, :]
            for d in range(3):
                value = value + xr[t, d, rows, :].astype(F32)
            zf[t, i] = value
            zs[t, i] = value.astype(BF16)
            return carry

        lax.fori_loop(0, 8, block, 0)
        for d in (4, 3, 5, 2, 6, 1, 7):
            to = (z + d) % 8
            send(zs.at[t, to], zr.at[t, d - 1], z_ss.at[t, d - 1], z_rs.at[t, d - 1], z_peer(d))

    def sum_z(t):
        for d in range(1, 8):
            arrived(zr.at[t, d - 1], z_ss.at[t, d - 1], z_rs.at[t, d - 1])
        value = zf[t, z]
        for d in range(7):
            value = value + zr[t, d].astype(F32)
        ps[t] = value.astype(BF16)
        send(ps.at[t], pr.at[t], p_ss.at[t], p_rs.at[t], y_pair)

    def send_z(t, origin, step, distance):
        piece = eg.at[t, r, (z - origin) % 8]
        send(piece, piece, az_ss.at[t, distance - 1], az_rs.at[t, distance - 1], z_peer(step))

    def arrived_z(t, d):
        arrived(eg.at[t, r, (z - d) % 8], az_ss.at[t, d - 1], az_rs.at[t, d - 1])

    def relay_z(t):
        arrived_z(t, 2)
        if t % 2 == 0:
            send_z(t, 2, 2, 4)
        send_z(t, 2, 1, 3)
        arrived_z(t, 6)
        if t % 2 == 1:
            send_z(t, 6, 6, 4)
        send_z(t, 6, 7, 5)

    def sum_pair(t):
        arrived(pr.at[t], p_ss.at[t], p_rs.at[t])
        value = ps[t].astype(F32) + pr[t].astype(F32) + dec_b[t : t + 1, :]
        ef[t] = value
        eg[t, r, z] = value.astype(BF16)
        err_out[t] = ef[t, pl.ds(pl.multiple_of(yl * 8, 8), 8), :].astype(BF16)
        for d in (4, 3, 5, 2, 6, 1, 7) if t in DIRECT_Z else (2, 6, 1, 7):
            send_z(t, 0, d, d)

    def gather_z(t):
        for d in (1, 2, 3, 4, 5, 6, 7) if t in DIRECT_Z else (1, 3, 4, 5, 7):
            arrived_z(t, d)
        for d in (2, 1, 3) if t in DIRECT_X else (1, 3):
            send(eg.at[t, r], eg.at[t, r], ax_ss.at[t, d - 1], ax_rs.at[t, d - 1], x_peer(d))

    first_z, last_z = pl.ds(0, 4), pl.ds(4, 4)

    def pass_on(t):
        for d, part, slot in ((1, first_z, 0), (3, last_z, 1)):
            chunk = (r - d) % 4
            arrived(eg.at[t, chunk], ax_ss.at[t, d - 1], ax_rs.at[t, d - 1])
            piece = eg.at[t, chunk, part]
            send(piece, piece, ay_ss.at[t, slot], ay_rs.at[t, slot], x_peer(d))

    def gradient(t, d):
        chunk = (r - d) % 4
        if d == 2:
            if t in DIRECT_X:
                arrived(eg.at[t, chunk], ax_ss.at[t, 1], ax_rs.at[t, 1])
            for part, slot in () if t in DIRECT_X else ((first_z, 0), (last_z, 1)):
                arrived(eg.at[t, chunk, part], ay_ss.at[t, slot], ay_rs.at[t, slot])
        elif d and t in DIRECT_X:
            arrived(eg.at[t, chunk], ax_ss.at[t, d - 1], ax_rs.at[t, d - 1])
        errors = eg[t, chunk].reshape(128, 576)
        for s in range(t, -1, -1):
            value = dot(errors, dv[pair_index(s, t)])
            if t < 3:
                value = value + acc[s, d]
            acc[s, d] = value
            if s == t:
                gs[s, d] = value.astype(BF16)

    def core_copy(s, d):
        return pltpu.make_async_remote_copy(
            src_ref=gs.at[s, d], dst_ref=ga.at[s, d], send_sem=gc_ss.at[s, d], recv_sem=gc_rs.at[s, d],
            device_id=core_peer, device_id_type=MESH,
        )

    def far_copy(s, d):
        return pltpu.make_async_remote_copy(
            src_ref=gt.at[s, d], dst_ref=gb.at[d], send_sem=gy_ss.at[s, d], recv_sem=gy_rs.at[s, d],
            device_id=far_peer, device_id_type=MESH,
        )

    def core_send(s, d):
        @pl.when(c != s % 2)
        def _():
            core_copy(s, d).start()

    def core_sum(s, d):
        @pl.when(c == s % 2)
        def _():
            core_copy(s, d).wait_recv()
            value = acc[s, d] + ga[s, d].astype(F32)
            acc[s, d] = value
            gt[s, d] = value.astype(BF16)

            @pl.when(yh != s // 2)
            def _():
                far_copy(s, d).start()

    def finish(s, d):
        @pl.when(l == s)
        def _():
            far_copy(s, d).wait_recv()
            rows = pl.ds(pl.multiple_of(((r - d) % 4) * 128, 128), 128)
            act_out[rows, :] = (acc[s, d] + gb[d].astype(F32)).astype(BF16)

        @pl.when(c != s % 2)
        def _():
            core_copy(s, d).wait_send()

        @pl.when((c == s % 2) & (yh != s // 2))
        def _():
            far_copy(s, d).wait_send()

    share(0)
    relay(1)
    relay(3)
    rest(1)
    share(1)
    hand_on(0)
    relay(2)
    rest(3)
    share(3)
    rest(2)
    share(2)
    hand_on(1)
    loads[5].wait()
    for i, peer_l in enumerate((core_l, far_l, cross_l)):
        arrived(wd.at[peer_l], w_ss.at[i], w_rs.at[i])
    have(0)
    decode(0, (3, 2))
    hand_on(3)
    have(1)
    decode(1, (3, 2))
    have(3)
    decode(3, (3, 2))
    hand_on(2)
    have(2)
    decode(2, (3, 2))
    decode(1, (1, 0))
    decode(3, (1, 0))
    decode(2, (1, 0))
    decode(0, (1, 0))
    sum_x(3)
    sum_x(2)
    sum_z(3)
    sum_pair(3)
    sum_z(2)
    sum_pair(2)
    gather_z(3)
    sum_x(1)
    gather_z(2)
    sum_x(0)
    sum_z(1)
    sum_pair(1)
    pass_on(3)
    sum_z(0)
    sum_pair(0)
    gather_z(1)
    pass_on(2)
    gather_z(0)
    order = (0, 1, 3, 2)

    def step(t, d):
        gradient(t, d)
        core_send(t, d)

    step(3, 0)
    step(3, 1)
    step(3, 3)
    step(3, 2)
    step(2, 0)
    core_sum(3, 0)
    step(2, 1)
    core_sum(3, 1)
    step(2, 3)
    core_sum(3, 3)
    step(2, 2)
    core_sum(3, 2)
    for d in order:
        step(1, d)
        core_sum(2, d)
    for i, d in enumerate(order):
        step(0, d)
        core_sum(1, d)
        if i:
            core_sum(0, order[i - 1])
    core_sum(0, 2)
    for s in (3, 2, 1, 0):
        for d in order:
            finish(s, d)
    for copy in pending:
        copy.wait_send()


def write_out(errors, grads, err_out, act_out):
    err_out[...] = jnp.stack([errors[t].astype(F32) for t in range(4)], axis=1).astype(BF16)
    act_out[...] = grads[...]


def body(resid, norm_gain, gate_weight, up_weight, down_weight, enc_weight, enc_bias, dec_weight, dec_bias):
    any_spec = pl.BlockSpec(memory_space=pl.ANY)
    vmem_spec = pl.BlockSpec(memory_space=pltpu.VMEM)
    vmem = pltpu.VMEM
    dma = pltpu.SemaphoreType.DMA
    scratch = [
        vmem((128, 2304), BF16),
        vmem((2, 4, 128, 1152), BF16),
        vmem((2304, 512), BF16),
        vmem((144, 2304), BF16),
        vmem((144, 2304), BF16),
        vmem((144, 2304), BF16),
        vmem((4, 144, 576), BF16),
        vmem((4, 144, 576), BF16),
        vmem((10, 576, 512), BF16),
        vmem((4, 4, 128, 512), BF16),
        vmem((4, 3, 128, 576), BF16),
        vmem((4, 128, 576), F32),
        vmem((4, 3, 128, 576), BF16),
        vmem((4, 8, 16, 576), F32),
        vmem((4, 8, 16, 576), BF16),
        vmem((4, 7, 16, 576), BF16),
        vmem((4, 16, 576), BF16),
        vmem((4, 16, 576), BF16),
        vmem((4, 16, 576), F32),
        vmem((4, 4, 8, 16, 576), BF16),
        vmem((4, 4, 128, 512), F32),
        vmem((4, 4, 128, 512), BF16),
        vmem((4, 4, 128, 512), BF16),
        vmem((4, 4, 128, 512), BF16),
        vmem((4, 128, 512), BF16),
        dma((6,)),
    ]
    for shape in ((3,), (3,), (2,), (3, 2), (4,), (4,), (4,), (4, 3), (4, 7), (4,), (4, 7), (4, 3), (4, 2), (4, 4), (4, 4)):
        scratch += [dma(shape), dma(shape)]
    scratch += [vmem((4, 4, 144, 128), BF16)] + [dma((4,)) for _ in range(6)]
    errors, act_grad = pl.pallas_call(
        kernel,
        out_shape=(
            jax.ShapeDtypeStruct((4, 8, 576), BF16),
            jax.ShapeDtypeStruct((512, 512), BF16),
        ),
        in_specs=[any_spec, vmem_spec, any_spec, any_spec, any_spec, any_spec, vmem_spec, any_spec, vmem_spec],
        out_specs=(vmem_spec, vmem_spec),
        scratch_shapes=scratch,
        compiler_params=pltpu.CompilerParams(
            collective_id=1, has_side_effects=True, vmem_limit_bytes=60 * 2**20
        ),
        cost_estimate=pl.CostEstimate(flops=8_200_000_000, bytes_accessed=12_000_000, transcendentals=100_000),
    )(
        resid[0], norm_gain, gate_weight[0], up_weight[0], down_weight[0], enc_weight[0], enc_bias,
        jnp.swapaxes(dec_weight, 1, 2), dec_bias,
    )
    return pl.pallas_call(
        write_out,
        out_shape=(jax.ShapeDtypeStruct((8, 4, 576), BF16), jax.ShapeDtypeStruct((1, 512, 512), BF16)),
        in_specs=[vmem_spec, vmem_spec],
        out_specs=(vmem_spec, vmem_spec),
    )(errors, act_grad[None])


def solution(mesh):
    in_specs = (
        P("layer", "rows", None),
        P("layer", None),
        P("layer", ("rows", "feat"), None),
        P("layer", ("rows", "feat"), None),
        P("layer", ("rows", "feat"), None),
        P("layer", None, ("rows", "feat")),
        P("layer", ("rows", "feat")),
        P(None, ("rows", "feat"), "layer"),
        P(None, "layer"),
    )
    out_specs = (P(("rows", "feat"), None, "layer"), P("layer", None, ("rows", "feat")))
    return jax.shard_map(body, mesh=mesh, in_specs=in_specs, out_specs=out_specs, check_vma=False)
```

```python
import jax
import jax.numpy as jnp
from jax import lax
from jax.experimental import pallas as pl
from jax.experimental.pallas import tpu as pltpu
from jax.sharding import PartitionSpec as P

MESH = pl.DeviceIdType.MESH
BF16 = jnp.bfloat16
F32 = jnp.float32
DIRECT_Z = (3, 2, 1, 0)
DIRECT_X = (0,)


def pair_index(source, target, layers=4):
    return source * layers - source * (source - 1) // 2 + target - source


def dot(left, right):
    return lax.dot_general(left, right, (((1,), (0,)), ((), ())), preferred_element_type=F32)


def dot_t(left, right):
    return lax.dot_general(left, right, (((1,), (1,)), ((), ())), preferred_element_type=F32)


def gelu(x):
    inner = 0.7978845608028654 * (x + 0.044715 * (x * x * x))
    return 0.5 * x * (1.0 + jnp.tanh(inner))


def kernel(
    resid, gain, gate_w, up_w, down_w, enc_w, enc_b, dec_w, dec_b,
    err_out, act_out,
    res_v, xg, ew, gw, uw, dw, wsend, wd, dv, fh,
    xs, own, xr, zf, zs, zr, ps, pr, ef, eg, acc, gs, ga, gt, gb,
    load_sem, w_ss, w_rs, xa_ss, xa_rs, xb_ss, xb_rs, zf_ss, zf_rs, fc_ss, fc_rs, fy_ss, fy_rs, ff_ss, ff_rs,
    x_ss, x_rs, z_ss, z_rs, p_ss, p_rs, az_ss, az_rs, ax_ss, ax_rs, ay_ss, ay_rs, gc_ss, gc_rs, gy_ss, gy_rs,
    hh, hy_ss, hy_rs, hc_ss, hc_rs, hf_ss, hf_rs,
):
    l, r, f = lax.axis_index("layer"), lax.axis_index("rows"), lax.axis_index("feat")
    yh, c = l // 2, l % 2
    z, yl = f // 2, f % 2
    half = z % 2
    other = 1 - half

    def x_peer(d):
        return (l, (r + d) % 4, f)

    def z_peer(d):
        return (l, r, ((z + d) % 8) * 2 + yl)

    y_pair = (l, r, z * 2 + (1 - yl))
    core_l = yh * 2 + (1 - c)
    far_l = (1 - yh) * 2 + c
    cross_l = (1 - yh) * 2 + (1 - c)
    core_peer, far_peer, cross_peer = (core_l, r, f), (far_l, r, f), (cross_l, r, f)

    pending = []

    def send(src, dst, ss, rs, peer):
        copy = pltpu.make_async_remote_copy(
            src_ref=src, dst_ref=dst, send_sem=ss, recv_sem=rs, device_id=peer, device_id_type=MESH
        )
        copy.start()
        pending.append(copy)

    def arrived(dst, ss, rs):
        pltpu.make_async_remote_copy(
            src_ref=dst, dst_ref=dst, send_sem=ss, recv_sem=rs, device_id=core_peer, device_id_type=MESH
        ).wait_recv()

    loads = [
        pltpu.make_async_copy(src, dst, load_sem.at[i])
        for i, (src, dst) in enumerate(
            ((resid, res_v), (down_w, dw), (enc_w, ew), (gate_w, gw), (up_w, uw), (dec_w, dv))
        )
    ]
    for copy in loads:
        copy.start()
    barrier = pltpu.get_barrier_semaphore()
    peers = [x_peer(d) for d in (1, 2, 3)] + [z_peer(d) for d in range(1, 8)]
    peers += [y_pair, core_peer, far_peer, cross_peer]
    for peer in peers:
        pl.semaphore_signal(barrier, inc=1, device_id=peer, device_id_type=MESH)

    loads[0].wait()

    def norm_rows(i, carry):
        rows = pl.ds(pl.multiple_of(i * 16, 16), 16)
        value = res_v[rows, :].astype(F32)
        inv = lax.rsqrt(jnp.mean(value * value, axis=-1, keepdims=True) + 1e-06)
        out = (value * inv * gain[...]).astype(BF16)
        xg[0, r, rows, :] = out[:, :1152]
        xg[1, r, rows, :] = out[:, 1152:]
        return carry

    lax.fori_loop(0, 8, norm_rows, 0)
    pl.semaphore_wait(barrier, len(peers))
    for d in (1, 3):
        send(xg.at[half, r], xg.at[half, r], xa_ss.at[d - 1], xa_rs.at[d - 1], x_peer(d))

    loads[1].wait()
    for q in range(4):
        wsend[q] = dw[:, q * 576 : (q + 1) * 576]
    for i, (peer_l, peer) in enumerate(((core_l, core_peer), (far_l, far_peer), (cross_l, cross_peer))):
        send(wsend.at[peer_l], wd.at[l], w_ss.at[i], w_rs.at[i], peer)
    wd[l] = wsend[l]

    for copy in loads[2:5]:
        copy.wait()

    def features(chunk):
        left, right = xg[0, chunk], xg[1, chunk]
        pre = dot(left, ew[:1152]) + dot(right, ew[1152:]) + enc_b[...]
        fh[l, chunk] = jnp.maximum(pre, 0.0).astype(BF16)
        gate = dot_t(gw[:, :1152], left) + dot_t(gw[:, 1152:], right)
        up = dot_t(uw[:, :1152], left) + dot_t(uw[:, 1152:], right)
        hh[l, chunk] = (gelu(gate) * up).astype(BF16)

    def share(d):
        chunk = (r - d) % 4
        features(chunk)
        send(fh.at[l, chunk], fh.at[l, chunk], fy_ss.at[d], fy_rs.at[d], far_peer)
        send(hh.at[l, chunk], hh.at[l, chunk], hy_ss.at[d], hy_rs.at[d], far_peer)
        send(fh.at[l, chunk], fh.at[l, chunk], fc_ss.at[d], fc_rs.at[d], core_peer)
        send(hh.at[l, chunk], hh.at[l, chunk], hc_ss.at[d], hc_rs.at[d], core_peer)

    def hand_on(d):
        chunk = (r - d) % 4
        arrived(fh.at[far_l, chunk], fy_ss.at[d], fy_rs.at[d])
        arrived(hh.at[far_l, chunk], hy_ss.at[d], hy_rs.at[d])
        send(fh.at[far_l, chunk], fh.at[far_l, chunk], ff_ss.at[d], ff_rs.at[d], core_peer)
        send(hh.at[far_l, chunk], hh.at[far_l, chunk], hf_ss.at[d], hf_rs.at[d], core_peer)

    def have(d):
        chunk = (r - d) % 4
        arrived(fh.at[core_l, chunk], fc_ss.at[d], fc_rs.at[d])
        arrived(hh.at[core_l, chunk], hc_ss.at[d], hc_rs.at[d])
        arrived(fh.at[cross_l, chunk], ff_ss.at[d], ff_rs.at[d])
        arrived(hh.at[cross_l, chunk], hf_ss.at[d], hf_rs.at[d])

    low, high = pl.ds(0, 64), pl.ds(64, 64)

    def relay(d):
        chunk = (r - d) % 4
        parts = ((low, 1, 0, 1), (high, 3, 1, 7))
        if d != 2:
            arrived(xg.at[half, chunk], xa_ss.at[d - 1], xa_rs.at[d - 1])
            part, step, slot, _ = parts[d // 2]
            piece = xg.at[half, chunk, part]
            send(piece, piece, xb_ss.at[slot], xb_rs.at[slot], x_peer(step))
        for part, _, slot, z_step in parts:
            piece = xg.at[half, chunk, part]
            if d == 2:
                arrived(piece, xb_ss.at[slot], xb_rs.at[slot])
            send(piece, piece, zf_ss.at[d - 1, slot], zf_rs.at[d - 1, slot], z_peer(z_step))

    def rest(d):
        chunk = (r - d) % 4
        arrived(xg.at[other, chunk, low], zf_ss.at[d - 1, 0], zf_rs.at[d - 1, 0])
        arrived(xg.at[other, chunk, high], zf_ss.at[d - 1, 1], zf_rs.at[d - 1, 1])

    def partial_sum(t, chunk):
        total = -lax.dot_general(
            hh[t, chunk], wd[t], (((0,), (0,)), ((), ())), preferred_element_type=F32
        )
        for s in range(t + 1):
            total = total + dot_t(fh[s, chunk], dv[pair_index(s, t)])
        return total

    def decode(d, targets):
        chunk = (r - d) % 4
        for t in targets:
            if d:
                xs[t, d - 1] = partial_sum(t, chunk).astype(BF16)
                send(xs.at[t, d - 1], xr.at[t, d - 1], x_ss.at[t, d - 1], x_rs.at[t, d - 1], x_peer(4 - d))
            else:
                own[t] = partial_sum(t, chunk)

    def sum_x(t):
        for d in (1, 3, 2):
            arrived(xr.at[t, d - 1], x_ss.at[t, d - 1], x_rs.at[t, d - 1])

        def block(i, carry):
            rows = pl.ds(pl.multiple_of(i * 16, 16), 16)
            value = own[t, rows, :]
            for d in range(3):
                value = value + xr[t, d, rows, :].astype(F32)
            zf[t, i] = value
            zs[t, i] = value.astype(BF16)
            return carry

        lax.fori_loop(0, 8, block, 0)
        for d in (4, 3, 5, 2, 6, 1, 7):
            to = (z + d) % 8
            send(zs.at[t, to], zr.at[t, d - 1], z_ss.at[t, d - 1], z_rs.at[t, d - 1], z_peer(d))

    def sum_z(t):
        for d in range(1, 8):
            arrived(zr.at[t, d - 1], z_ss.at[t, d - 1], z_rs.at[t, d - 1])
        value = zf[t, z]
        for d in range(7):
            value = value + zr[t, d].astype(F32)
        ps[t] = value.astype(BF16)
        send(ps.at[t], pr.at[t], p_ss.at[t], p_rs.at[t], y_pair)

    def send_z(t, origin, step, distance):
        piece = eg.at[t, r, (z - origin) % 8]
        send(piece, piece, az_ss.at[t, distance - 1], az_rs.at[t, distance - 1], z_peer(step))

    def arrived_z(t, d):
        arrived(eg.at[t, r, (z - d) % 8], az_ss.at[t, d - 1], az_rs.at[t, d - 1])

    def relay_z(t):
        arrived_z(t, 2)
        if t % 2 == 0:
            send_z(t, 2, 2, 4)
        send_z(t, 2, 1, 3)
        arrived_z(t, 6)
        if t % 2 == 1:
            send_z(t, 6, 6, 4)
        send_z(t, 6, 7, 5)

    def sum_pair(t):
        arrived(pr.at[t], p_ss.at[t], p_rs.at[t])
        value = ps[t].astype(F32) + pr[t].astype(F32) + dec_b[t : t + 1, :]
        ef[t] = value
        eg[t, r, z] = value.astype(BF16)
        err_out[t] = ef[t, pl.ds(pl.multiple_of(yl * 8, 8), 8), :].astype(BF16)
        for d in (4, 3, 5, 2, 6, 1, 7) if t in DIRECT_Z else (2, 6, 1, 7):
            send_z(t, 0, d, d)

    def gather_z(t):
        for d in (1, 2, 3, 4, 5, 6, 7) if t in DIRECT_Z else (1, 3, 4, 5, 7):
            arrived_z(t, d)
        for d in (2, 1, 3) if t in DIRECT_X else (1, 3):
            send(eg.at[t, r], eg.at[t, r], ax_ss.at[t, d - 1], ax_rs.at[t, d - 1], x_peer(d))

    first_z, last_z = pl.ds(0, 4), pl.ds(4, 4)

    def pass_on(t):
        for d, part, slot in ((1, first_z, 0), (3, last_z, 1)):
            chunk = (r - d) % 4
            arrived(eg.at[t, chunk], ax_ss.at[t, d - 1], ax_rs.at[t, d - 1])
            piece = eg.at[t, chunk, part]
            send(piece, piece, ay_ss.at[t, slot], ay_rs.at[t, slot], x_peer(d))

    def gradient(t, d):
        chunk = (r - d) % 4
        if d == 2:
            if t in DIRECT_X:
                arrived(eg.at[t, chunk], ax_ss.at[t, 1], ax_rs.at[t, 1])
            for part, slot in () if t in DIRECT_X else ((first_z, 0), (last_z, 1)):
                arrived(eg.at[t, chunk, part], ay_ss.at[t, slot], ay_rs.at[t, slot])
        elif d and t in DIRECT_X:
            arrived(eg.at[t, chunk], ax_ss.at[t, d - 1], ax_rs.at[t, d - 1])
        errors = eg[t, chunk].reshape(128, 576)
        for s in range(t, -1, -1):
            value = dot(errors, dv[pair_index(s, t)])
            if t < 3:
                value = value + acc[s, d]
            acc[s, d] = value
            if s == t:
                gs[s, d] = value.astype(BF16)

    def core_copy(s, d):
        return pltpu.make_async_remote_copy(
            src_ref=gs.at[s, d], dst_ref=ga.at[s, d], send_sem=gc_ss.at[s, d], recv_sem=gc_rs.at[s, d],
            device_id=core_peer, device_id_type=MESH,
        )

    def far_copy(s, d):
        return pltpu.make_async_remote_copy(
            src_ref=gt.at[s, d], dst_ref=gb.at[d], send_sem=gy_ss.at[s, d], recv_sem=gy_rs.at[s, d],
            device_id=far_peer, device_id_type=MESH,
        )

    def core_send(s, d):
        @pl.when(c != s % 2)
        def _():
            core_copy(s, d).start()

    def core_sum(s, d):
        @pl.when(c == s % 2)
        def _():
            core_copy(s, d).wait_recv()
            value = acc[s, d] + ga[s, d].astype(F32)
            acc[s, d] = value
            gt[s, d] = value.astype(BF16)

            @pl.when(yh != s // 2)
            def _():
                far_copy(s, d).start()

    def finish(s, d):
        @pl.when(l == s)
        def _():
            far_copy(s, d).wait_recv()
            rows = pl.ds(pl.multiple_of(((r - d) % 4) * 128, 128), 128)
            act_out[rows, :] = (acc[s, d] + gb[d].astype(F32)).astype(BF16)

        @pl.when(c != s % 2)
        def _():
            core_copy(s, d).wait_send()

        @pl.when((c == s % 2) & (yh != s // 2))
        def _():
            far_copy(s, d).wait_send()

    order = (0, 1, 3, 2)

    def step(t, d):
        gradient(t, d)
        core_send(t, d)

    share(0)
    relay(1)
    relay(3)
    rest(1)
    share(1)
    hand_on(0)
    relay(2)
    rest(3)
    share(3)
    rest(2)
    share(2)
    hand_on(1)
    loads[5].wait()
    for i, peer_l in enumerate((core_l, far_l, cross_l)):
        arrived(wd.at[peer_l], w_ss.at[i], w_rs.at[i])
    have(0)
    decode(0, (3, 2))
    hand_on(3)
    have(1)
    decode(1, (3, 2))
    have(3)
    decode(3, (3, 2))
    hand_on(2)
    have(2)
    decode(2, (3, 2))
    decode(1, (1, 0))
    decode(3, (1, 0))
    decode(2, (1, 0))
    decode(0, (1, 0))
    sum_x(3)
    sum_x(2)
    sum_z(3)
    sum_pair(3)
    sum_z(2)
    sum_pair(2)
    gather_z(3)
    sum_x(1)
    gather_z(2)
    step(3, 0)
    sum_x(0)
    sum_z(1)
    sum_pair(1)
    pass_on(3)
    sum_z(0)
    step(2, 0)
    sum_pair(0)
    gather_z(1)
    pass_on(2)
    step(3, 1)
    gather_z(0)
    step(3, 3)
    pass_on(1)
    step(3, 2)
    core_sum(3, 0)
    step(2, 1)
    core_sum(3, 1)
    step(2, 3)
    core_sum(3, 3)
    step(2, 2)
    core_sum(3, 2)
    for d in order:
        step(1, d)
        core_sum(2, d)
    for i, d in enumerate(order):
        step(0, d)
        core_sum(1, d)
        if i:
            core_sum(0, order[i - 1])
    core_sum(0, 2)
    for s in (3, 2, 1, 0):
        for d in order:
            finish(s, d)
    for copy in pending:
        copy.wait_send()


def write_out(errors, grads, err_out, act_out):
    err_out[...] = jnp.stack([errors[t].astype(F32) for t in range(4)], axis=1).astype(BF16)
    act_out[...] = grads[...]


def body(resid, norm_gain, gate_weight, up_weight, down_weight, enc_weight, enc_bias, dec_weight, dec_bias):
    any_spec = pl.BlockSpec(memory_space=pl.ANY)
    vmem_spec = pl.BlockSpec(memory_space=pltpu.VMEM)
    vmem = pltpu.VMEM
    dma = pltpu.SemaphoreType.DMA
    scratch = [
        vmem((128, 2304), BF16),
        vmem((2, 4, 128, 1152), BF16),
        vmem((2304, 512), BF16),
        vmem((144, 2304), BF16),
        vmem((144, 2304), BF16),
        vmem((144, 2304), BF16),
        vmem((4, 144, 576), BF16),
        vmem((4, 144, 576), BF16),
        vmem((10, 576, 512), BF16),
        vmem((4, 4, 128, 512), BF16),
        vmem((4, 3, 128, 576), BF16),
        vmem((4, 128, 576), F32),
        vmem((4, 3, 128, 576), BF16),
        vmem((4, 8, 16, 576), F32),
        vmem((4, 8, 16, 576), BF16),
        vmem((4, 7, 16, 576), BF16),
        vmem((4, 16, 576), BF16),
        vmem((4, 16, 576), BF16),
        vmem((4, 16, 576), F32),
        vmem((4, 4, 8, 16, 576), BF16),
        vmem((4, 4, 128, 512), F32),
        vmem((4, 4, 128, 512), BF16),
        vmem((4, 4, 128, 512), BF16),
        vmem((4, 4, 128, 512), BF16),
        vmem((4, 128, 512), BF16),
        dma((6,)),
    ]
    for shape in ((3,), (3,), (2,), (3, 2), (4,), (4,), (4,), (4, 3), (4, 7), (4,), (4, 7), (4, 3), (4, 2), (4, 4), (4, 4)):
        scratch += [dma(shape), dma(shape)]
    scratch += [vmem((4, 4, 144, 128), BF16)] + [dma((4,)) for _ in range(6)]
    errors, act_grad = pl.pallas_call(
        kernel,
        out_shape=(
            jax.ShapeDtypeStruct((4, 8, 576), BF16),
            jax.ShapeDtypeStruct((512, 512), BF16),
        ),
        in_specs=[any_spec, vmem_spec, any_spec, any_spec, any_spec, any_spec, vmem_spec, any_spec, vmem_spec],
        out_specs=(vmem_spec, vmem_spec),
        scratch_shapes=scratch,
        compiler_params=pltpu.CompilerParams(
            collective_id=1, has_side_effects=True, vmem_limit_bytes=60 * 2**20
        ),
        cost_estimate=pl.CostEstimate(flops=8_200_000_000, bytes_accessed=12_000_000, transcendentals=100_000),
    )(
        resid[0], norm_gain, gate_weight[0], up_weight[0], down_weight[0], enc_weight[0], enc_bias,
        jnp.swapaxes(dec_weight, 1, 2), dec_bias,
    )
    return pl.pallas_call(
        write_out,
        out_shape=(jax.ShapeDtypeStruct((8, 4, 576), BF16), jax.ShapeDtypeStruct((1, 512, 512), BF16)),
        in_specs=[vmem_spec, vmem_spec],
        out_specs=(vmem_spec, vmem_spec),
    )(errors, act_grad[None])


def solution(mesh):
    in_specs = (
        P("layer", "rows", None),
        P("layer", None),
        P("layer", ("rows", "feat"), None),
        P("layer", ("rows", "feat"), None),
        P("layer", ("rows", "feat"), None),
        P("layer", None, ("rows", "feat")),
        P("layer", ("rows", "feat")),
        P(None, ("rows", "feat"), "layer"),
        P(None, "layer"),
    )
    out_specs = (P(("rows", "feat"), None, "layer"), P("layer", None, ("rows", "feat")))
    return jax.shard_map(body, mesh=mesh, in_specs=in_specs, out_specs=out_specs, check_vma=False)
```
